128 devices in a mesh: section: 16 (over z, x), tensor: 8 (over y, core).
Axes of the slice: x: 4, y: 4, z: 4, core: 2. Of those that a mesh axis runs over, the one named last changes fastest.
Arguments:
- prompt_rows: bfloat16 [32768, 8192], P('section'), may hold values from -10 to 10
- page_slot: int32 [16, 16, 8], P('section'), may hold values from -1 to 63, as said below
- context_len: int32 [128], P('section'), may hold values from 1 to 128, as said below
- new_tokens: bfloat16 [2, 128, 8192], P(None, None, 'section'), may hold values from -26 to 26
- norm_gain: float32 [8192], replicated, may hold values from 0.25 to 1.75
- q_weight: bfloat16 [8192, 8192], P('section', 'tensor'), may hold values from -1 to 1
- kv_weight: bfloat16 [8192, 2048], P('section', 'tensor'), may hold values from -1 to 1
- o_weight: bfloat16 [8192, 8192], P('tensor', 'section'), may hold values from -0.0625 to 0.0625
Outputs:
- layer_out: bfloat16 [2, 128, 8192], P(None, 'tensor', 'section')
The draws below stay inside these ranges and needn't reach their ends.
Inputs may be any that keep to these rules, and one draw needn't show every extreme that they name: page_slot[s, g, c] = j * 8 + p says that slot c of section s holds page p of sequence j of decode group g; -1 marks an empty slot. Each of the 64 pages of every group sits in exactly one slot, and for every group some section fills all 8 of its slots. `context_len`: in every group of 8 sequences one sequence has the full 8 * 16 tokens.
All inputs are finite; a program needn't handle non-finite values.
Results may differ from the reference program's by a relative error of at most 0.0051.
Values may be sent and summed in bfloat16 or wider, within the bound.
No kernel may reach another device: no remote copies, remote signals or barrier semaphores. Data moves between devices by JAX's collectives and lax.ppermute only.
A program may use at most 128 MiB of HBM per device.

```python
import math
import jax
import jax.numpy as jnp
from jax import lax

D = 8192
HQ = 64
KVH = 8
HD = 128
GQ = 8
PAGE = 16
CAP = 8
SEQ_G = 8
PAGES_SEQ = 8
BATCH = 128
ROWS_DEV = 2048
ROWS = 32768
N_SECTION = 16


def draw_prompt_rows(key, part):
    key = jax.random.fold_in(key, 5)
    key_main = jax.random.fold_in(key, 0)
    drawn = jnp.clip(jax.random.normal(key_main, (ROWS, D), jnp.float32), -6.0, 6.0)
    return drawn.astype(jnp.bfloat16)


def draw_q_weight(key, part):
    key = jax.random.fold_in(key, 41)
    key_noise = jax.random.fold_in(key, 0)
    drawn = jnp.clip(jax.random.normal(key_noise, (D, HQ * HD), jnp.float32), -4.0, 4.0) * D ** (-0.5)
    return drawn.astype(jnp.bfloat16)


def draw_kv_weight(key, part):
    key = jax.random.fold_in(key, 43)
    drawn = jnp.clip(jax.random.normal(key, (D, 2 * KVH * HD), jnp.float32), -4.0, 4.0) * D ** (-0.5)
    return drawn.astype(jnp.bfloat16)


def draw_page_slot(key, part):
    key = jax.random.fold_in(key, 11)
    slots = N_SECTION * CAP
    live = SEQ_G * PAGES_SEQ

    def one_dest(dest_key):
        key_full, key_score, key_perm = jax.random.split(dest_key, 3)
        full_owner = jax.random.randint(key_full, (), 0, N_SECTION)
        index = jnp.arange(slots, dtype=jnp.int32)
        owner = index // CAP
        score = jax.random.randint(key_score, (slots,), 0, 1 << 16) * slots + index
        score = jnp.where(owner == full_owner, index - slots, score)
        order = jnp.argsort(score)
        ranking = jnp.argsort(order).astype(jnp.int32)
        labels = jax.random.permutation(key_perm, live).astype(jnp.int32)
        chosen = labels[jnp.minimum(ranking, live - 1)]
        return jnp.where(ranking < live, chosen, -1).reshape(N_SECTION, CAP)
    table = jax.vmap(one_dest)(jax.random.split(key, N_SECTION))
    return jnp.transpose(table, (1, 0, 2)).astype(jnp.int32)


def draw_context_len(key, part):
    key = jax.random.fold_in(key, 23)
    key_len, key_pick = jax.random.split(key)
    longest = PAGES_SEQ * PAGE
    lengths = jax.random.randint(key_len, (N_SECTION, SEQ_G), 1, longest + 1)
    picked = jax.random.randint(key_pick, (N_SECTION, 1), 0, SEQ_G)
    lengths = jnp.where(jnp.arange(SEQ_G, dtype=jnp.int32)[None, :] == picked, longest, lengths)
    return lengths.reshape(BATCH).astype(jnp.int32)


def draw_new_tokens(key, part):
    key = jax.random.fold_in(key, 37)
    key_main = jax.random.fold_in(key, 0)
    column = jnp.arange(D, dtype=jnp.float32)
    rising = 1.0 + 2.0 * column / (D - 1)
    drawn = jnp.clip(jax.random.normal(key_main, (2, BATCH, D), jnp.float32), -4.0, 4.0) * rising
    return drawn.astype(jnp.bfloat16)


def block_scale(rng, shape, shards, least, top_value):
    level, own = 1.0, jax.random.fold_in(rng, 6)
    for axis_at, shards_of in shards:
        heights = jnp.exp(jax.random.uniform(jax.random.fold_in(own, axis_at), (shards_of,), jnp.float32, least / len(shards), top_value / len(shards)))
        level = level * jnp.repeat(heights, shape[axis_at] // shards_of).reshape([-1 if axis == axis_at else 1 for axis in range(len(shape))])
    return level


def centred(key, extent, width, reach, cuts=(), held_as=jnp.bfloat16):
    result = width * jax.random.normal(key, extent, jnp.float32)
    if cuts:
        result = result * block_scale(key, extent, cuts, -0.22, 0.18)
    return jnp.clip(result, -reach, reach).astype(held_as)


def setup_inputs(seed: int = 0) -> dict:
    seeds = jax.random.split(jax.random.key(seed), 9)
    prompt_rows = draw_prompt_rows(jax.random.fold_in(seeds[8], 71), 0)
    page_slot = draw_page_slot(jax.random.fold_in(seeds[8], 71), 0)
    context_len = draw_context_len(jax.random.fold_in(seeds[8], 71), 0)
    new_tokens = draw_new_tokens(jax.random.fold_in(seeds[8], 71), 0)
    norm_gain = jnp.clip(1.0 + 0.15 * jax.random.normal(seeds[4], (D,), jnp.float32), 0.25, 1.75)
    q_weight = draw_q_weight(jax.random.fold_in(seeds[8], 71), 0)
    kv_weight = draw_kv_weight(jax.random.fold_in(seeds[8], 71), 0)
    o_weight = centred(seeds[7], (HQ * HD, D), (HQ * HD) ** -0.5, 0.0625, ((0, 8), (1, 16)))
    return {"prompt_rows": prompt_rows, "page_slot": page_slot, "context_len": context_len, "new_tokens": new_tokens, "norm_gain": norm_gain, "q_weight": q_weight, "kv_weight": kv_weight, "o_weight": o_weight}


EPS = 1e-05
ROPE_BASE = 500000.0

def rotate(vectors, positions):
    half_dim = vectors.shape[-1] // 2
    frequency = ROPE_BASE ** (-2.0 * jnp.arange(half_dim, dtype=jnp.float32) / vectors.shape[-1])
    angles = positions.astype(jnp.float32)[..., None, None] * frequency
    first = vectors[..., :half_dim]
    second = vectors[..., half_dim:]
    cosine = jnp.cos(angles)
    sine_term = jnp.sin(angles)
    return jnp.concatenate([first * cosine - second * sine_term, second * cosine + first * sine_term], axis=-1)

def attend(queries, new_keys, new_values, keys, values, slot_ids, lengths, pages_seq):
    count = queries.shape[1]
    scale = 1.0 / math.sqrt(queries.shape[-1])
    offsets = jnp.arange(PAGE, dtype=jnp.int32)
    shape = slot_ids.shape + (PAGE,)
    seq_tok = jnp.broadcast_to((slot_ids // pages_seq)[..., None], shape).reshape(-1)
    pos_tok = ((slot_ids % pages_seq)[..., None] * PAGE + offsets).reshape(-1)
    valid = jnp.broadcast_to((slot_ids >= 0)[..., None], shape).reshape(-1)
    query_f32 = queries.astype(jnp.float32)
    scores = jnp.einsum('isjgh,ljh->isjgl', query_f32, keys.astype(jnp.float32)) * scale
    new_scores = jnp.einsum('isjgh,tsjh->isjgt', query_f32, new_keys.astype(jnp.float32)) * scale
    owners = jnp.arange(count, dtype=jnp.int32)
    cache_mask = (valid[None, :] & (seq_tok[None, :] == owners[:, None]) & (pos_tok[None, :] < lengths[:, None]))[None, :, None, None, :]
    steps = jnp.arange(2, dtype=jnp.int32)
    step_mask = (steps[None, :] <= steps[:, None])[:, None, None, None, :]
    highest = jnp.maximum(lax.optimization_barrier(jnp.max(jnp.where(cache_mask, scores, -jnp.inf), axis=-1)), lax.optimization_barrier(jnp.max(jnp.where(step_mask, new_scores, -jnp.inf), axis=-1)))[..., None]
    cache_exp = jnp.where(cache_mask, jnp.exp(scores - highest), 0.0)
    step_exp = jnp.where(step_mask, jnp.exp(new_scores - highest), 0.0)
    denom_sum = lax.optimization_barrier(jnp.sum(cache_exp, axis=-1, keepdims=True)) + lax.optimization_barrier(jnp.sum(step_exp, axis=-1, keepdims=True))
    cache_weight = (cache_exp / denom_sum).astype(jnp.bfloat16)
    step_weight = (step_exp / denom_sum).astype(jnp.bfloat16)
    mixed = jnp.einsum('isjgl,ljh->isjgh', cache_weight.astype(jnp.float32), values.astype(jnp.float32))
    mixed = mixed + jnp.einsum('isjgt,tsjh->isjgh', step_weight.astype(jnp.float32), new_values.astype(jnp.float32))
    return mixed.reshape(2, count, -1).astype(jnp.bfloat16)

def reference(prompt_rows, page_slot, context_len, new_tokens, norm_gain, q_weight, kv_weight, o_weight):

    def prefill(block):
        block_f32 = block.astype(jnp.float32)
        normed = (block_f32 * lax.rsqrt(lax.optimization_barrier(jnp.mean(block_f32 * block_f32, axis=-1, keepdims=True)) + EPS) * norm_gain).astype(jnp.bfloat16)
        return jnp.dot(normed, kv_weight, preferred_element_type=jnp.float32)
    prompt_kv = lax.map(prefill, prompt_rows.reshape(N_SECTION, ROWS_DEV, D))
    prompt_kv = prompt_kv.reshape(N_SECTION, N_SECTION, CAP, PAGE, KVH, 2, HD)
    slot_clamped = jnp.maximum(page_slot, 0)
    positions = (slot_clamped % PAGES_SEQ)[..., None] * PAGE + jnp.arange(PAGE, dtype=jnp.int32)
    cache_keys = rotate(prompt_kv[..., 0, :], positions).astype(jnp.bfloat16)
    cache_values = prompt_kv[..., 1, :].astype(jnp.bfloat16)
    token_f32 = new_tokens.astype(jnp.float32)
    scaled = (token_f32 * norm_gain).astype(jnp.bfloat16).reshape(2 * BATCH, D)
    rscale = lax.rsqrt(lax.optimization_barrier(jnp.mean(token_f32 * token_f32, axis=-1, keepdims=True)) + EPS)
    new_positions = context_len[None, :] + jnp.arange(2, dtype=jnp.int32)[:, None]
    query_proj = jnp.dot(scaled, q_weight, preferred_element_type=jnp.float32).reshape(2, BATCH, HQ * HD) * rscale
    queries = rotate(query_proj.reshape(2, BATCH, HQ, HD), new_positions).astype(jnp.bfloat16)
    kv_proj = (jnp.dot(scaled, kv_weight, preferred_element_type=jnp.float32).reshape(2, BATCH, 2 * KVH * HD) * rscale).reshape(2, BATCH, KVH, 2, HD)
    new_keys = rotate(kv_proj[..., 0, :], new_positions).astype(jnp.bfloat16)
    new_values = kv_proj[..., 1, :].astype(jnp.bfloat16)
    group_queries = jnp.moveaxis(queries.reshape(2, N_SECTION, SEQ_G, KVH, GQ, HD), 1, 0)
    group_keys = jnp.moveaxis(new_keys.reshape(2, N_SECTION, SEQ_G, KVH, HD), 1, 0)
    group_values = jnp.moveaxis(new_values.reshape(2, N_SECTION, SEQ_G, KVH, HD), 1, 0)
    keys_by_group = jnp.moveaxis(cache_keys, 1, 0).reshape(N_SECTION, N_SECTION * CAP * PAGE, KVH, HD)
    values_by_group = jnp.moveaxis(cache_values, 1, 0).reshape(N_SECTION, N_SECTION * CAP * PAGE, KVH, HD)
    slot_ids = jnp.moveaxis(page_slot, 1, 0)
    lengths = context_len.reshape(N_SECTION, SEQ_G)

    def one_group(items):
        return attend(items[0], items[1], items[2], items[3], items[4], items[5], items[6], PAGES_SEQ)
    attn = lax.map(one_group, (group_queries, group_keys, group_values, keys_by_group, values_by_group, slot_ids, lengths))
    attn = jnp.moveaxis(attn, 0, 1).reshape(2 * BATCH, HQ * HD)
    output = token_f32 + jnp.dot(attn, o_weight, preferred_element_type=jnp.float32).reshape(2, BATCH, D)
    return output.astype(jnp.bfloat16)
```

```python
import functools
import math

import jax
import jax.numpy as jnp
from jax import lax
from jax.experimental import pallas as pl
from jax.experimental.pallas import tpu as pltpu
from jax.sharding import PartitionSpec as P

D = 8192
HD = 128
GQ = 8
PAGE = 16
CAP = 8
SEQ_G = 8
SECTIONS = 16
GROUP_TOK = CAP * PAGE
ROWS = 2 * SEQ_G
DEPTH = D // SECTIONS
WQ = GQ * HD
WKV = 2 * HD
EXTRA = 128
ID_LANE = 8
POSITIONS = 136

EPS = 1e-05
ROPE_BASE = 500000.0
BF16 = jnp.bfloat16
F32 = jnp.float32
VMEM_LIMIT = 40 * 1024 * 1024


def params(**more):
    return pltpu.CompilerParams(vmem_limit_bytes=VMEM_LIMIT, **more)


def rotation_tables():
    half = HD // 2
    frequency = ROPE_BASE ** (-2.0 * jnp.arange(half, dtype=F32) / HD)
    angles = jnp.arange(POSITIONS, dtype=jnp.int32).astype(F32)[:, None] * frequency
    cosine, sine = jnp.cos(angles), jnp.sin(angles)
    return (
        jnp.concatenate([cosine, cosine], axis=-1),
        jnp.concatenate([-sine, sine], axis=-1),
    )


def turned(rows, cosine, sine):
    return rows * cosine + pltpu.roll(rows, HD // 2, 1) * sine


def shifted(array, axis, step):
    pairs = []
    for z in range(4):
        for x in range(4):
            for member in range(8):
                along_x = (axis + member) % 2 == 0
                to_z = z if along_x else (z + step) % 4
                to_x = (x + step) % 4 if along_x else x
                pairs.append(((z * 4 + x) * 8 + member, (to_z * 4 + to_x) * 8 + member))
    return lax.ppermute(array, ("section", "tensor"), pairs)


def prompt_kernel(first, last, *refs):
    if last:
        _, ids_ref, *refs = refs
    else:
        _, *refs = refs
    x_refs, refs = refs[:4], refs[4:]
    wa_ref, wb_ref, *refs = refs
    if not first:
        acc_ref, squares_ref, *refs = refs
    if last:
        cos_ref, sin_ref, pages_ref = refs
    else:
        acc_out, squares_out = refs

    total, squares = None, None
    for k, x_ref in enumerate(x_refs):
        x = x_ref[...]
        w_ref = (wa_ref, wb_ref)[k // 2]
        w = w_ref[(k % 2) * DEPTH : (k % 2 + 1) * DEPTH, :]
        part = jnp.dot(x, w, preferred_element_type=F32)
        total = part if total is None else total + part
        wide = x.astype(F32)
        wide = wide * wide
        for c in range(DEPTH // 128):
            piece = wide[:, c * 128 : (c + 1) * 128]
            squares = piece if squares is None else squares + piece
    if not first:
        total = total + acc_ref[...]
        squares = squares + squares_ref[...]
    if not last:
        acc_out[...] = total
        squares_out[...] = squares
        return
    mean = jnp.sum(squares, axis=-1, keepdims=True) * (1.0 / D)
    total = total * lax.rsqrt(mean + EPS)
    groups = total.shape[0] // GROUP_TOK
    for g in range(groups):
        group = pl.program_id(0) * groups + g
        for c in range(CAP):
            row = g * GROUP_TOK + c * PAGE
            page = jnp.maximum(ids_ref[group, c], 0) % CAP
            at = pl.ds(pl.multiple_of(page * PAGE, PAGE), PAGE)
            key = turned(total[row : row + PAGE, :HD], cos_ref[at, :], sin_ref[at, :])
            pages_ref[g, c * PAGE : (c + 1) * PAGE, :HD] = key.astype(BF16)
        pages_ref[g, :, HD:] = total[g * GROUP_TOK : (g + 1) * GROUP_TOK, HD:].astype(BF16)


def prompt_pass(x, blocks, wa, wb, carry=None, final=None):
    first, last = carry is None, final is not None
    rows = x.shape[0]
    step = 512
    n_scalars = 2 if last else 1

    def x_at(k):
        return pl.BlockSpec((step, DEPTH), lambda r, blocks, *_: (r, blocks[k]))

    whole_w = pl.BlockSpec((2 * DEPTH, WKV), lambda r, *_: (0, 0))
    acc_spec = pl.BlockSpec((step, WKV), lambda r, *_: (r, 0))
    sq_spec = pl.BlockSpec((step, 128), lambda r, *_: (r, 0))
    in_specs = [x_at(k) for k in range(4)] + [whole_w, whole_w]
    args = [x] * 4 + [wa, wb]
    if not first:
        in_specs += [acc_spec, sq_spec]
        args += list(carry)
    scalars = [blocks]
    if last:
        ids, cosine, sine = final
        scalars.append(ids)
        table = pl.BlockSpec((POSITIONS, HD), lambda r, *_: (0, 0))
        in_specs += [table, table]
        args += [cosine, sine]
        groups = step // GROUP_TOK
        out_specs = pl.BlockSpec((groups, GROUP_TOK, WKV), lambda r, *_: (r, 0, 0))
        out_shape = jax.ShapeDtypeStruct((rows // GROUP_TOK, GROUP_TOK, WKV), BF16)
    else:
        out_specs = [acc_spec, sq_spec]
        out_shape = [
            jax.ShapeDtypeStruct((rows, WKV), F32),
            jax.ShapeDtypeStruct((rows, 128), F32),
        ]
    return pl.pallas_call(
        functools.partial(prompt_kernel, first, last),
        grid_spec=pltpu.PrefetchScalarGridSpec(
            num_scalar_prefetch=n_scalars,
            grid=(rows // step,),
            in_specs=in_specs,
            out_specs=out_specs,
        ),
        out_shape=out_shape,
        compiler_params=params(),
        name="prompt_last" if last else "prompt_first" if first else "prompt_middle",
    )(*scalars, *args)


def project_kernel(tok_ref, gain_ref, qw_ref, kvw_ref, ids_ref, out_ref):
    tok = tok_ref[...].astype(F32)
    scaled = (tok * gain_ref[...]).astype(BF16)
    squares = jnp.sum(tok * tok, axis=-1, keepdims=True)
    high = squares.astype(BF16).astype(F32)
    low = squares - high
    q = jnp.dot(scaled, qw_ref[...], preferred_element_type=F32)
    kv = jnp.dot(scaled, kvw_ref[...], preferred_element_type=F32)
    lane = lax.broadcasted_iota(jnp.int32, (tok.shape[0], EXTRA), 1)
    extra = jnp.where(lane == 0, high, jnp.where(lane == 1, low, 0.0))
    half = tok.shape[0] // 2
    for g in range(SECTIONS):
        ids = ids_ref[g : g + 1, :]
        for array, at, width in ((q, 0, WQ), (kv, WQ, WKV), (extra, WQ + WKV, EXTRA)):
            rows = jnp.concatenate(
                [
                    array[g * SEQ_G : (g + 1) * SEQ_G],
                    array[half + g * SEQ_G : half + (g + 1) * SEQ_G],
                ],
                axis=0,
            )
            if width == EXTRA:
                rows = rows + ids
            out_ref[g, :, at : at + width] = rows.astype(BF16)


def project(tokens, gain, q_weight, kv_weight, ids_wide):
    return pl.pallas_call(
        project_kernel,
        out_shape=jax.ShapeDtypeStruct((SECTIONS, ROWS, WQ + WKV + EXTRA), BF16),
        compiler_params=params(),
        name="project",
    )(tokens, gain, q_weight, kv_weight, ids_wide)


def ready_kernel(ctx_ref, got_ref, cos_ref, sin_ref, q_ref, key_ref, value_ref, seq_ref):
    got = got_ref[...].astype(F32)
    total = jnp.sum(got, axis=0)
    squares = (
        total[:, WQ + WKV : WQ + WKV + 1] + total[:, WQ + WKV + 1 : WQ + WKV + 2]
    )
    rscale = lax.rsqrt(squares * (1.0 / D) + EPS)
    total = total[:, : WQ + WKV] * rscale
    cosine = jnp.concatenate(
        [cos_ref[pl.ds(ctx_ref[r % SEQ_G] + r // SEQ_G, 1), :] for r in range(ROWS)], axis=0
    )
    sine = jnp.concatenate(
        [sin_ref[pl.ds(ctx_ref[r % SEQ_G] + r // SEQ_G, 1), :] for r in range(ROWS)], axis=0
    )
    for h in range(GQ):
        q_ref[h * ROWS : (h + 1) * ROWS, :] = turned(
            total[:, h * HD : (h + 1) * HD], cosine, sine
        ).astype(BF16)
    key_ref[...] = turned(total[:, WQ : WQ + HD], cosine, sine).astype(BF16)
    value_ref[...] = total[:, WQ + HD : WQ + WKV].astype(BF16)

    ids = jnp.max(got[:, :, WQ + WKV :], axis=1)
    lane_in = lax.broadcasted_iota(jnp.int32, (EXTRA, GROUP_TOK), 0)
    lane_out = lax.broadcasted_iota(jnp.int32, (EXTRA, GROUP_TOK), 1)
    spread = (lane_in == ID_LANE + lane_out // PAGE).astype(F32)
    ids = jnp.where(
        (lax.broadcasted_iota(jnp.int32, ids.shape, 1) >= ID_LANE), ids, 0.0
    )
    ids = jnp.dot(ids, spread, preferred_element_type=F32).astype(jnp.int32)
    position = (ids & (CAP - 1)) * PAGE + (
        lax.broadcasted_iota(jnp.int32, ids.shape, 1) & (PAGE - 1)
    )
    owner = jnp.full(ids.shape, -1, jnp.int32)
    for j in range(SEQ_G):
        held = (ids >= j * CAP) & (ids < (j + 1) * CAP) & (position < ctx_ref[j])
        owner = jnp.where(held, j, owner)
    seq_ref[...] = owner


def ready(context_len, got, cosine, sine):
    vmem = pl.BlockSpec(memory_space=pltpu.VMEM)
    return pl.pallas_call(
        ready_kernel,
        in_specs=[pl.BlockSpec(memory_space=pltpu.SMEM), vmem, vmem, vmem],
        out_shape=[
            jax.ShapeDtypeStruct((GQ * ROWS, HD), BF16),
            jax.ShapeDtypeStruct((ROWS, HD), BF16),
            jax.ShapeDtypeStruct((ROWS, HD), BF16),
            jax.ShapeDtypeStruct((SECTIONS, GROUP_TOK), jnp.int32),
        ],
        compiler_params=params(),
        name="ready",
    )(context_len, got, cosine, sine)


def attend_kernel(pages_ref, q_ref, key_ref, value_ref, seq_ref, out_ref):
    scale = 1.0 / math.sqrt(HD)
    q = q_ref[...]
    n = GQ * ROWS

    def against(keys):
        return (
            lax.dot_general(q, keys, (((1,), (1,)), ((), ())), preferred_element_type=F32) * scale
        )

    row = lax.broadcasted_iota(jnp.int32, (n, 1), 0)
    row_seq, row_step = row & (SEQ_G - 1), (row // SEQ_G) & 1
    col = lax.broadcasted_iota(jnp.int32, (n, ROWS), 1)
    fresh_ok = ((col & (SEQ_G - 1)) == row_seq) & (col // SEQ_G <= row_step)
    fresh = jnp.where(fresh_ok, against(key_ref[...]), -jnp.inf)
    cached = []
    peak = None
    for s in range(SECTIONS):
        ok = seq_ref[s : s + 1, :] == row_seq
        scores = jnp.where(ok, against(pages_ref[s, :, :HD]), -jnp.inf)
        cached.append(scores)
        peak = scores if peak is None else jnp.maximum(peak, scores)
    highest = jnp.maximum(
        jnp.max(peak, axis=-1, keepdims=True), jnp.max(fresh, axis=-1, keepdims=True)
    )
    fresh = jnp.exp(fresh - highest)
    cached = [jnp.exp(scores - highest) for scores in cached]
    denom = cached[0]
    for scores in cached[1:]:
        denom = denom + scores
    denom = jnp.sum(denom, axis=-1, keepdims=True) + jnp.sum(fresh, axis=-1, keepdims=True)
    inverse = 1.0 / denom
    mixed = jnp.dot(
        (fresh * inverse).astype(BF16), value_ref[...], preferred_element_type=F32
    )
    for s in range(SECTIONS):
        mixed = mixed + jnp.dot(
            (cached[s] * inverse).astype(BF16), pages_ref[s, :, HD:], preferred_element_type=F32
        )
    mixed = mixed.astype(BF16)
    for d in range(SECTIONS):
        for h in range(GQ):
            out_ref[d, :, h * HD : (h + 1) * HD] = mixed[h * ROWS : (h + 1) * ROWS]


def attend(pages, q, key, value, seq):
    return pl.pallas_call(
        attend_kernel,
        out_shape=jax.ShapeDtypeStruct((SECTIONS, ROWS, WQ), BF16),
        compiler_params=params(),
        name="attend",
    )(pages, q, key, value, seq)


def output_kernel(attn_ref, ow_ref, out_ref):
    attn = attn_ref[...].reshape(SECTIONS * ROWS, WQ)
    part = jnp.dot(attn, ow_ref[...], preferred_element_type=F32)
    out_ref[...] = part.astype(BF16).reshape(out_ref.shape)


def output_part(attn, o_weight, members):
    return pl.pallas_call(
        output_kernel,
        out_shape=jax.ShapeDtypeStruct(
            (members, SECTIONS * ROWS // members, o_weight.shape[1]), BF16
        ),
        compiler_params=params(),
        name="output_part",
    )(attn, o_weight)


def finish_kernel(_, got_ref, tok_ref, out_ref):
    total = jnp.sum(got_ref[...].astype(F32), axis=0)
    tok = tok_ref[...].astype(F32)
    for i in range(2):
        rows = jnp.concatenate(
            [total[g * ROWS + i * SEQ_G : g * ROWS + (i + 1) * SEQ_G] for g in range(2)], axis=0
        )
        out_ref[i] = (tok[i] + rows).astype(BF16)


def finish(member, got, tokens):
    members, rows, width = got.shape
    block = pl.BlockSpec((2, rows // 2, width), lambda r, member: (0, member[0], 0))
    return pl.pallas_call(
        finish_kernel,
        grid_spec=pltpu.PrefetchScalarGridSpec(
            num_scalar_prefetch=1,
            grid=(1,),
            in_specs=[pl.BlockSpec(got.shape, lambda r, member: (0, 0, 0)), block],
            out_specs=pl.BlockSpec((2, rows // 2, width), lambda r, member: (0, 0, 0)),
        ),
        out_shape=jax.ShapeDtypeStruct((2, rows // 2, width), BF16),
        compiler_params=params(),
        name="finish",
    )(member, got, tokens)


def on_device(
    prompt_rows, page_slot, context_len, new_tokens, norm_gain, q_weight, kv_weight, o_weight
):
    section = lax.axis_index("section")
    member = lax.axis_index("tensor")
    members = lax.axis_size("tensor")
    core = member % 2
    own_ids = page_slot[0]
    gain_here = lax.dynamic_slice_in_dim(norm_gain, section * DEPTH, DEPTH, 0)
    cosine, sine = rotation_tables()

    weight = (kv_weight.astype(F32) * gain_here[:, None]).astype(BF16)
    from_1 = shifted(weight, 0, 1)
    from_3 = shifted(weight, 0, -1)
    from_2 = shifted(weight, 0, 2)
    near = jnp.concatenate([weight, from_1], axis=0)
    far = jnp.concatenate([from_3, from_2], axis=0)
    near_p = shifted(near, 1, 1)
    far_m = shifted(far, 1, -1)
    near_2, far_2 = lax.optimization_barrier((near, far))
    far_p = shifted(far_2, 1, 1)
    near_m = shifted(near_2, 1, -1)
    near_o = shifted(near_p, 1, 1)
    far_o = shifted(far_m, 1, -1)

    def blocks(*steps):
        z, x = section // 4, section % 4
        ids = []
        for a, b in steps:
            at_0 = ((z + b) % 4) * 4 + (x + a) % 4
            at_1 = ((z + a) % 4) * 4 + (x + b) % 4
            ids.append(jnp.where(core == 0, at_0, at_1))
        return jnp.stack(ids).astype(jnp.int32)

    ids_wide = jnp.pad(
        own_ids.astype(F32), ((0, 0), (ID_LANE, EXTRA - ID_LANE - CAP))
    )
    payload = project(
        new_tokens.reshape(-1, DEPTH), gain_here[None, :], q_weight, kv_weight, ids_wide
    )
    got = lax.all_to_all(payload, "section", split_axis=0, concat_axis=0, tiled=True)
    queries, new_keys, new_values, owners = ready(context_len, got, cosine, sine)

    carry = prompt_pass(
        prompt_rows, blocks((0, 0), (3, 0), (1, 0), (2, 0)), near, far
    )
    carry = prompt_pass(
        prompt_rows, blocks((0, 3), (3, 3), (1, 1), (2, 1)), near_p, far_m, carry
    )
    carry = prompt_pass(
        prompt_rows, blocks((0, 1), (3, 1), (1, 3), (2, 3)), near_m, far_p, carry
    )
    pages = prompt_pass(
        prompt_rows,
        blocks((0, 2), (3, 2), (1, 2), (2, 2)),
        near_o,
        far_o,
        carry,
        (own_ids, cosine, sine),
    )
    received = lax.all_to_all(pages, "section", split_axis=0, concat_axis=0, tiled=True)
    attn = attend(received, queries, new_keys, new_values, owners)
    attn = lax.all_to_all(attn, "section", split_axis=0, concat_axis=0, tiled=True)
    part = output_part(attn, o_weight, members)
    part = lax.all_to_all(part, "tensor", split_axis=0, concat_axis=0, tiled=True)
    return finish(member[None].astype(jnp.int32), part, new_tokens)


def solution(mesh):
    placed = (
        P("section", None),
        P("section", None, None),
        P("section"),
        P(None, None, "section"),
        P(),
        P("section", "tensor"),
        P("section", "tensor"),
        P("tensor", "section"),
    )
    return jax.shard_map(
        on_device,
        mesh=mesh,
        in_specs=placed,
        out_specs=P(None, "tensor", "section"),
        check_vma=False,
    )
```

```python
import functools
import math

import jax
import jax.numpy as jnp
from jax import lax
from jax.experimental import pallas as pl
from jax.experimental.pallas import tpu as pltpu
from jax.sharding import PartitionSpec as P

D = 8192
HD = 128
GQ = 8
PAGE = 16
CAP = 8
SEQ_G = 8
SECTIONS = 16
GROUP_TOK = CAP * PAGE
ROWS = 2 * SEQ_G
DEPTH = D // SECTIONS
WQ = GQ * HD
WKV = 2 * HD
EXTRA = 128
ID_LANE = 8
POSITIONS = 136

EPS = 1e-05
ROPE_BASE = 500000.0
BF16 = jnp.bfloat16
F32 = jnp.float32


def params(mib=16):
    return pltpu.CompilerParams(vmem_limit_bytes=mib * 1024 * 1024)


def rotation_tables():
    half = HD // 2
    frequency = ROPE_BASE ** (-2.0 * jnp.arange(half, dtype=F32) / HD)
    angles = jnp.arange(POSITIONS, dtype=jnp.int32).astype(F32)[:, None] * frequency
    cosine, sine = jnp.cos(angles), jnp.sin(angles)
    return (
        jnp.concatenate([cosine, cosine], axis=-1),
        jnp.concatenate([-sine, sine], axis=-1),
    )


def turned(rows, cosine, sine):
    return rows * cosine + pltpu.roll(rows, HD // 2, 1) * sine


def shifted(array, axis, step):
    pairs = []
    for z in range(4):
        for x in range(4):
            for member in range(8):
                along_x = (axis + member) % 2 == 0
                to_z = z if along_x else (z + step) % 4
                to_x = (x + step) % 4 if along_x else x
                pairs.append(((z * 4 + x) * 8 + member, (to_z * 4 + to_x) * 8 + member))
    return lax.ppermute(array, ("section", "tensor"), pairs)


TILE = 256
PAGES = TILE // PAGE
BUFFERS = 3


def early_kernel(n_early, blocks_ref, order_ref, count_ref, x_ref, *refs):
    w_refs, refs = refs[: n_early // 2], refs[n_early // 2 :]
    acc_ref, rest_ref, squares_ref, buf_ref, sems = refs
    count = count_ref[0]

    def copy(t, c):
        slot = t % BUFFERS
        row = pl.multiple_of(order_ref[t * PAGES + c] * PAGE, PAGE)
        return pltpu.make_async_copy(
            x_ref.at[pl.ds(row, PAGE), :],
            buf_ref.at[slot, pl.ds(c * PAGE, PAGE), :],
            sems.at[slot, c],
        )

    def begin(t):
        for c in range(PAGES):

            @pl.when(t * PAGES + c < count)
            def _():
                copy(t, c).start()

    def end(t):
        for c in range(PAGES):

            @pl.when(t * PAGES + c < count)
            def _():
                copy(t, c).wait()

    for t in range(BUFFERS - 1):
        begin(t)

    def tile(t, _):
        begin(t + BUFFERS - 1)
        end(t)
        slot = t % BUFFERS
        rows = pl.ds(pl.multiple_of(t * TILE, TILE), TILE)

        def depth(k):
            return pl.ds(pl.multiple_of(blocks_ref[k] * DEPTH, DEPTH), DEPTH)

        total = None
        for k in range(n_early):
            w = w_refs[k // 2][(k % 2) * DEPTH : (k % 2 + 1) * DEPTH, :]
            part = jnp.dot(buf_ref[slot, :, depth(k)], w, preferred_element_type=F32)
            total = part if total is None else total + part
        acc_ref[rows, :] = total
        for k in range(n_early, SECTIONS):
            at = (k - n_early) * DEPTH
            rest_ref[rows, at : at + DEPTH] = buf_ref[slot, :, depth(k)]
        for c in range(PAGES):
            sums = [None] * 4
            for j in range(D // 128):
                piece = buf_ref[slot, c * PAGE : (c + 1) * PAGE, j * 128 : (j + 1) * 128]
                piece = piece.astype(F32)
                piece = piece * piece
                sums[j % 4] = piece if sums[j % 4] is None else sums[j % 4] + piece
            at = pl.multiple_of(t * TILE + c * PAGE, PAGE)
            squares_ref[pl.ds(at, PAGE), :] = (sums[0] + sums[1]) + (sums[2] + sums[3])
        return 0

    lax.fori_loop(0, pl.cdiv(count, PAGES), tile, 0)


def kept(array):
    return pltpu.with_memory_space_constraint(array, pltpu.VMEM)


def in_hbm(array):
    return pltpu.with_memory_space_constraint(array, pltpu.HBM)


SMEM_SPEC = pl.BlockSpec(memory_space=pltpu.SMEM)
VMEM_SPEC = pl.BlockSpec(memory_space=pltpu.VMEM)


def prompt_early(blocks, order, count, x, weights):
    rows = x.shape[0]
    n_early = 2 * len(weights)
    return pl.pallas_call(
        functools.partial(early_kernel, n_early),
        in_specs=[SMEM_SPEC] * 3
        + [pl.BlockSpec(memory_space=pl.ANY)]
        + [VMEM_SPEC] * len(weights),
        out_specs=[VMEM_SPEC] * 3,
        out_shape=[
            pltpu.VMEM((rows, WKV), F32),
            pltpu.VMEM((rows, (SECTIONS - n_early) * DEPTH), BF16),
            pltpu.VMEM((rows, 128), F32),
        ],
        scratch_shapes=[
            pltpu.VMEM((BUFFERS, TILE, D), BF16),
            pltpu.SemaphoreType.DMA((BUFFERS, PAGES)),
        ],
        compiler_params=params(24),
        name="prompt_early",
    )(blocks, order, count, x, *weights)


def late_kernel(
    order_ref, turn_ref, count_ref, cos_ref, sin_ref, acc_ref, rest_ref, squares_ref, *refs
):
    w_refs, (pages_ref, tile_ref, cos_tile, sin_tile) = refs[:-4], refs[-4:]
    count = count_ref[0]
    pages_ref[...] = jnp.zeros_like(pages_ref)

    def tile(t, _):
        rows = pl.ds(pl.multiple_of(t * TILE, TILE), TILE)
        last = count - 1 - t * PAGES
        for c in range(PAGES):
            page = turn_ref[t * PAGES + jnp.minimum(c, last)]
            turn = pl.ds(pl.multiple_of(page * PAGE, PAGE), PAGE)
            cos_tile[c * PAGE : (c + 1) * PAGE, :] = cos_ref[turn, :]
            sin_tile[c * PAGE : (c + 1) * PAGE, :] = sin_ref[turn, :]
        total = acc_ref[rows, :]
        for k, w_ref in enumerate(w_refs):
            x = rest_ref[rows, k * 2 * DEPTH : (k + 1) * 2 * DEPTH]
            total = total + jnp.dot(x, w_ref[...], preferred_element_type=F32)
        mean = jnp.sum(squares_ref[rows, :], axis=-1, keepdims=True) * (1.0 / D)
        total = total * lax.rsqrt(mean + EPS)
        tile_ref[:, :HD] = turned(total[:, :HD], cos_tile[...], sin_tile[...]).astype(BF16)
        tile_ref[:, HD:] = total[:, HD:].astype(BF16)
        for c in range(PAGES):
            source = jnp.minimum(c, last)
            slot = order_ref[t * PAGES + source]
            to = pl.ds(pl.multiple_of((slot % CAP) * PAGE, PAGE), PAGE)
            here = pl.ds(pl.multiple_of(source * PAGE, PAGE), PAGE)
            pages_ref[slot // CAP, to, :] = tile_ref[here, :]
        return 0

    lax.fori_loop(0, pl.cdiv(count, PAGES), tile, 0)


def prompt_late(order, turn, count, cosine, sine, early, weights):
    return pl.pallas_call(
        late_kernel,
        in_specs=[SMEM_SPEC] * 3 + [VMEM_SPEC] * (5 + len(weights)),
        out_specs=VMEM_SPEC,
        out_shape=jax.ShapeDtypeStruct((SECTIONS, GROUP_TOK, WKV), BF16),
        scratch_shapes=[
            pltpu.VMEM((TILE, WKV), BF16),
            pltpu.VMEM((TILE, HD), F32),
            pltpu.VMEM((TILE, HD), F32),
        ],
        compiler_params=params(16),
        name="prompt_late",
    )(order, turn, count, cosine, sine, *[kept(array) for array in early], *weights)


def project_kernel(
    slot_ref, tok_ref, gain_ref, qw_ref, kvw_ref, ids_ref, out_ref, order_ref, turn_ref, count_ref
):
    found = jnp.int32(0)
    for slot in range(SECTIONS * CAP):
        held = slot_ref[slot // CAP, slot % CAP]
        order_ref[found] = slot
        turn_ref[found] = jnp.maximum(held, 0) & (CAP - 1)
        found = found + jnp.where(held >= 0, 1, 0)
    count_ref[0] = found

    tok = tok_ref[...].astype(F32)
    scaled = (tok * gain_ref[...]).astype(BF16)
    squares = jnp.sum(tok * tok, axis=-1, keepdims=True)
    high = squares.astype(BF16).astype(F32)
    low = squares - high
    q = jnp.dot(scaled, qw_ref[...], preferred_element_type=F32)
    kv = jnp.dot(scaled, kvw_ref[...], preferred_element_type=F32)
    lane = lax.broadcasted_iota(jnp.int32, (tok.shape[0], EXTRA), 1)
    extra = jnp.where(lane == 0, high, jnp.where(lane == 1, low, 0.0))
    half = tok.shape[0] // 2
    for g in range(SECTIONS):
        ids = ids_ref[g : g + 1, :]
        for array, at, width in ((q, 0, WQ), (kv, WQ, WKV), (extra, WQ + WKV, EXTRA)):
            rows = jnp.concatenate(
                [
                    array[g * SEQ_G : (g + 1) * SEQ_G],
                    array[half + g * SEQ_G : half + (g + 1) * SEQ_G],
                ],
                axis=0,
            )
            if width == EXTRA:
                rows = rows + ids
            out_ref[g, :, at : at + width] = rows.astype(BF16)


def project(own_ids, tokens, gain, q_weight, kv_weight, ids_wide):
    slots = jax.ShapeDtypeStruct((SECTIONS * CAP,), jnp.int32)
    return pl.pallas_call(
        project_kernel,
        in_specs=[SMEM_SPEC] + [VMEM_SPEC] * 5,
        out_specs=[VMEM_SPEC] + [SMEM_SPEC] * 3,
        out_shape=[
            jax.ShapeDtypeStruct((SECTIONS, ROWS, WQ + WKV + EXTRA), BF16),
            slots,
            slots,
            jax.ShapeDtypeStruct((1,), jnp.int32),
        ],
        compiler_params=params(),
        name="project",
    )(own_ids, in_hbm(tokens), gain, in_hbm(q_weight), kv_weight, ids_wide)


def ready_kernel(ctx_ref, got_ref, cos_ref, sin_ref, q_ref, key_ref, value_ref, seq_ref):
    got = got_ref[...].astype(F32)
    total = jnp.sum(got, axis=0)
    squares = (
        total[:, WQ + WKV : WQ + WKV + 1] + total[:, WQ + WKV + 1 : WQ + WKV + 2]
    )
    rscale = lax.rsqrt(squares * (1.0 / D) + EPS)
    total = total[:, : WQ + WKV] * rscale
    cosine = jnp.concatenate(
        [cos_ref[pl.ds(ctx_ref[r % SEQ_G] + r // SEQ_G, 1), :] for r in range(ROWS)], axis=0
    )
    sine = jnp.concatenate(
        [sin_ref[pl.ds(ctx_ref[r % SEQ_G] + r // SEQ_G, 1), :] for r in range(ROWS)], axis=0
    )
    for h in range(GQ):
        q_ref[h * ROWS : (h + 1) * ROWS, :] = turned(
            total[:, h * HD : (h + 1) * HD], cosine, sine
        ).astype(BF16)
    key_ref[...] = turned(total[:, WQ : WQ + HD], cosine, sine).astype(BF16)
    value_ref[...] = total[:, WQ + HD : WQ + WKV].astype(BF16)

    ids = jnp.max(got[:, :, WQ + WKV :], axis=1)
    lane_in = lax.broadcasted_iota(jnp.int32, (EXTRA, GROUP_TOK), 0)
    lane_out = lax.broadcasted_iota(jnp.int32, (EXTRA, GROUP_TOK), 1)
    spread = (lane_in == ID_LANE + lane_out // PAGE).astype(F32)
    ids = jnp.where(
        (lax.broadcasted_iota(jnp.int32, ids.shape, 1) >= ID_LANE), ids, 0.0
    )
    ids = jnp.dot(ids, spread, preferred_element_type=F32).astype(jnp.int32)
    position = (ids & (CAP - 1)) * PAGE + (
        lax.broadcasted_iota(jnp.int32, ids.shape, 1) & (PAGE - 1)
    )
    owner = jnp.full(ids.shape, -1, jnp.int32)
    for j in range(SEQ_G):
        held = (ids >= j * CAP) & (ids < (j + 1) * CAP) & (position < ctx_ref[j])
        owner = jnp.where(held, j, owner)
    seq_ref[...] = owner


def ready(context_len, got, cosine, sine):
    vmem = pl.BlockSpec(memory_space=pltpu.VMEM)
    return pl.pallas_call(
        ready_kernel,
        in_specs=[pl.BlockSpec(memory_space=pltpu.SMEM), vmem, vmem, vmem],
        out_shape=[
            jax.ShapeDtypeStruct((GQ * ROWS, HD), BF16),
            jax.ShapeDtypeStruct((ROWS, HD), BF16),
            jax.ShapeDtypeStruct((ROWS, HD), BF16),
            jax.ShapeDtypeStruct((SECTIONS, GROUP_TOK), jnp.int32),
        ],
        compiler_params=params(),
        name="ready",
    )(context_len, got, cosine, sine)


def attend_kernel(pages_ref, q_ref, key_ref, value_ref, seq_ref, ow_ref, out_ref, ow_out, sem):
    fetch = pltpu.make_async_copy(ow_ref, ow_out, sem)
    fetch.start()
    scale = 1.0 / math.sqrt(HD)
    q = q_ref[...]
    n = GQ * ROWS

    def against(keys):
        return (
            lax.dot_general(q, keys, (((1,), (1,)), ((), ())), preferred_element_type=F32) * scale
        )

    row = lax.broadcasted_iota(jnp.int32, (n, 1), 0)
    row_seq, row_step = row & (SEQ_G - 1), (row // SEQ_G) & 1
    col = lax.broadcasted_iota(jnp.int32, (n, ROWS), 1)
    fresh_ok = ((col & (SEQ_G - 1)) == row_seq) & (col // SEQ_G <= row_step)
    fresh = jnp.where(fresh_ok, against(key_ref[...]), -jnp.inf)
    cached = []
    peak = None
    for s in range(SECTIONS):
        ok = seq_ref[s : s + 1, :] == row_seq
        scores = jnp.where(ok, against(pages_ref[s, :, :HD]), -jnp.inf)
        cached.append(scores)
        peak = scores if peak is None else jnp.maximum(peak, scores)
    highest = jnp.maximum(
        jnp.max(peak, axis=-1, keepdims=True), jnp.max(fresh, axis=-1, keepdims=True)
    )
    fresh = jnp.exp(fresh - highest)
    cached = [jnp.exp(scores - highest) for scores in cached]
    denom = cached[0]
    for scores in cached[1:]:
        denom = denom + scores
    denom = jnp.sum(denom, axis=-1, keepdims=True) + jnp.sum(fresh, axis=-1, keepdims=True)
    inverse = 1.0 / denom
    mixed = jnp.dot(
        (fresh * inverse).astype(BF16), value_ref[...], preferred_element_type=F32
    )
    for s in range(SECTIONS):
        mixed = mixed + jnp.dot(
            (cached[s] * inverse).astype(BF16), pages_ref[s, :, HD:], preferred_element_type=F32
        )
    mixed = mixed.astype(BF16)
    for d in range(SECTIONS):
        for h in range(GQ):
            out_ref[d, :, h * HD : (h + 1) * HD] = mixed[h * ROWS : (h + 1) * ROWS]
    fetch.wait()


def attend(pages, q, key, value, seq, o_weight):
    return pl.pallas_call(
        attend_kernel,
        in_specs=[VMEM_SPEC] * 5 + [pl.BlockSpec(memory_space=pl.ANY)],
        out_specs=[VMEM_SPEC] * 2,
        out_shape=[
            jax.ShapeDtypeStruct((SECTIONS, ROWS, WQ), BF16),
            pltpu.VMEM(o_weight.shape, BF16),
        ],
        scratch_shapes=[pltpu.SemaphoreType.DMA(())],
        compiler_params=params(),
        name="attend",
    )(pages, q, key, value, seq, in_hbm(o_weight))


def output_kernel(attn_ref, ow_ref, out_ref):
    attn = attn_ref[...].reshape(SECTIONS * ROWS, WQ)
    part = jnp.dot(attn, ow_ref[...], preferred_element_type=F32)
    out_ref[...] = part.astype(BF16).reshape(out_ref.shape)


def output_part(attn, o_weight, members):
    return pl.pallas_call(
        output_kernel,
        out_shape=jax.ShapeDtypeStruct(
            (members, SECTIONS * ROWS // members, o_weight.shape[1]), BF16
        ),
        compiler_params=params(),
        name="output_part",
    )(attn, kept(o_weight))


def finish_kernel(_, got_ref, tok_ref, out_ref):
    total = jnp.sum(got_ref[...].astype(F32), axis=0)
    tok = tok_ref[...].astype(F32)
    for i in range(2):
        rows = jnp.concatenate(
            [total[g * ROWS + i * SEQ_G : g * ROWS + (i + 1) * SEQ_G] for g in range(2)], axis=0
        )
        out_ref[i] = (tok[i] + rows).astype(BF16)


def finish(member, got, tokens):
    members, rows, width = got.shape
    block = pl.BlockSpec((2, rows // 2, width), lambda r, member: (0, member[0], 0))
    return pl.pallas_call(
        finish_kernel,
        grid_spec=pltpu.PrefetchScalarGridSpec(
            num_scalar_prefetch=1,
            grid=(1,),
            in_specs=[pl.BlockSpec(got.shape, lambda r, member: (0, 0, 0)), block],
            out_specs=pl.BlockSpec((2, rows // 2, width), lambda r, member: (0, 0, 0)),
        ),
        out_shape=jax.ShapeDtypeStruct((2, rows // 2, width), BF16),
        compiler_params=params(),
        name="finish",
    )(member, got, tokens)


def on_device(
    prompt_rows, page_slot, context_len, new_tokens, norm_gain, q_weight, kv_weight, o_weight
):
    section = lax.axis_index("section")
    member = lax.axis_index("tensor")
    members = lax.axis_size("tensor")
    core = member % 2
    own_ids = page_slot[0]
    gain_here = lax.dynamic_slice_in_dim(norm_gain, section * DEPTH, DEPTH, 0)
    cosine, sine = rotation_tables()

    ids_wide = jnp.pad(own_ids.astype(F32), ((0, 0), (ID_LANE, EXTRA - ID_LANE - CAP)))
    payload, order, turn, count = project(
        own_ids, new_tokens.reshape(-1, DEPTH), gain_here[None, :], q_weight, kv_weight, ids_wide
    )

    weight = (kv_weight.astype(F32) * gain_here[:, None]).astype(BF16)
    from_1 = shifted(weight, 0, 1)
    from_3 = shifted(weight, 0, -1)
    from_2 = shifted(weight, 0, 2)
    near = jnp.concatenate([weight, from_1], axis=0)
    far = jnp.concatenate([from_3, from_2], axis=0)
    near, far, payload = lax.optimization_barrier((near, far, payload))
    got = lax.all_to_all(payload, "section", split_axis=0, concat_axis=0, tiled=True)
    near_p = shifted(near, 1, 1)
    far_m = shifted(far, 1, -1)
    near_2, far_2 = lax.optimization_barrier((near, far))
    far_p = shifted(far_2, 1, 1)
    near_m = shifted(near_2, 1, -1)
    near_o = shifted(near_p, 1, 1)
    far_o = shifted(far_m, 1, -1)

    def blocks(*steps):
        z, x = section // 4, section % 4
        ids = []
        for a, b in steps:
            at_0 = ((z + b) % 4) * 4 + (x + a) % 4
            at_1 = ((z + a) % 4) * 4 + (x + b) % 4
            ids.append(jnp.where(core == 0, at_0, at_1))
        return jnp.stack(ids).astype(jnp.int32)

    where = blocks(
        (0, 0), (3, 0), (1, 0), (2, 0),
        (0, 3), (3, 3), (1, 1), (2, 1),
        (0, 1), (3, 1), (1, 3), (2, 3),
        (0, 2), (3, 2), (1, 2), (2, 2),
    )
    early = prompt_early(where, order, count, prompt_rows, (near, far, near_p, far_m))
    pages = prompt_late(
        order, turn, count, cosine, sine, early, (near_m, far_p, near_o, far_o)
    )
    queries, new_keys, new_values, owners = ready(context_len, got, cosine, sine)
    received = lax.all_to_all(pages, "section", split_axis=0, concat_axis=0, tiled=True)
    attn, o_weight = attend(received, queries, new_keys, new_values, owners, o_weight)
    attn = lax.all_to_all(attn, "section", split_axis=0, concat_axis=0, tiled=True)
    part = output_part(attn, o_weight, members)
    part = lax.all_to_all(part, "tensor", split_axis=0, concat_axis=0, tiled=True)
    return finish(member[None].astype(jnp.int32), part, new_tokens)


def solution(mesh):
    placed = (
        P("section", None),
        P("section", None, None),
        P("section"),
        P(None, None, "section"),
        P(),
        P("section", "tensor"),
        P("section", "tensor"),
        P("tensor", "section"),
    )
    return jax.shard_map(
        on_device,
        mesh=mesh,
        in_specs=placed,
        out_specs=P(None, "tensor", "section"),
        check_vma=False,
    )
```

```python
import functools
import math

import jax
import jax.numpy as jnp
from jax import lax
from jax.experimental import pallas as pl
from jax.experimental.pallas import tpu as pltpu
from jax.sharding import PartitionSpec as P

D = 8192
HD = 128
GQ = 8
PAGE = 16
CAP = 8
SEQ_G = 8
SECTIONS = 16
GROUP_TOK = CAP * PAGE
ROWS = 2 * SEQ_G
DEPTH = D // SECTIONS
WQ = GQ * HD
WKV = 2 * HD
EXTRA = 128
ID_LANE = 8
POSITIONS = 136

EPS = 1e-05
ROPE_BASE = 500000.0
BF16 = jnp.bfloat16
F32 = jnp.float32


def params(mib=16):
    return pltpu.CompilerParams(vmem_limit_bytes=mib * 1024 * 1024)


def rotation_tables():
    half = HD // 2
    frequency = ROPE_BASE ** (-2.0 * jnp.arange(half, dtype=F32) / HD)
    angles = jnp.arange(POSITIONS, dtype=jnp.int32).astype(F32)[:, None] * frequency
    cosine, sine = jnp.cos(angles), jnp.sin(angles)
    return (
        jnp.concatenate([cosine, cosine], axis=-1),
        jnp.concatenate([-sine, sine], axis=-1),
    )


def turned(rows, cosine, sine):
    return rows * cosine + pltpu.roll(rows, HD // 2, 1) * sine


def shifted(array, axis, step):
    pairs = []
    for z in range(4):
        for x in range(4):
            for member in range(8):
                along_x = (axis + member) % 2 == 0
                to_z = z if along_x else (z + step) % 4
                to_x = (x + step) % 4 if along_x else x
                pairs.append(((z * 4 + x) * 8 + member, (to_z * 4 + to_x) * 8 + member))
    return lax.ppermute(array, ("section", "tensor"), pairs)


TILE = 256
PAGES = TILE // PAGE
BUFFERS = 3


def early_kernel(n_early, blocks_ref, order_ref, count_ref, x_ref, *refs):
    w_refs, refs = refs[: n_early // 2], refs[n_early // 2 :]
    acc_ref, rest_ref, squares_ref, buf_ref, sems = refs
    count = count_ref[0]

    def copy(t, c):
        slot = t % BUFFERS
        row = pl.multiple_of(order_ref[t * PAGES + c] * PAGE, PAGE)
        return pltpu.make_async_copy(
            x_ref.at[pl.ds(row, PAGE), :],
            buf_ref.at[slot, pl.ds(c * PAGE, PAGE), :],
            sems.at[slot, c],
        )

    def begin(t):
        for c in range(PAGES):

            @pl.when(t * PAGES + c < count)
            def _():
                copy(t, c).start()

    def end(t):
        for c in range(PAGES):

            @pl.when(t * PAGES + c < count)
            def _():
                copy(t, c).wait()

    for t in range(BUFFERS - 1):
        begin(t)

    def tile(t, _):
        begin(t + BUFFERS - 1)
        end(t)
        slot = t % BUFFERS
        rows = pl.ds(pl.multiple_of(t * TILE, TILE), TILE)

        def depth(k):
            return pl.ds(pl.multiple_of(blocks_ref[k] * DEPTH, DEPTH), DEPTH)

        total = None
        for k in range(n_early):
            w = w_refs[k // 2][(k % 2) * DEPTH : (k % 2 + 1) * DEPTH, :]
            part = jnp.dot(buf_ref[slot, :, depth(k)], w, preferred_element_type=F32)
            total = part if total is None else total + part
        acc_ref[rows, :] = total
        for k in range(n_early, SECTIONS):
            at = (k - n_early) * DEPTH
            rest_ref[rows, at : at + DEPTH] = buf_ref[slot, :, depth(k)]
        for c in range(PAGES):
            sums = [None] * 4
            for j in range(D // 128):
                piece = buf_ref[slot, c * PAGE : (c + 1) * PAGE, j * 128 : (j + 1) * 128]
                piece = piece.astype(F32)
                piece = piece * piece
                sums[j % 4] = piece if sums[j % 4] is None else sums[j % 4] + piece
            at = pl.multiple_of(t * TILE + c * PAGE, PAGE)
            squares_ref[pl.ds(at, PAGE), :] = (sums[0] + sums[1]) + (sums[2] + sums[3])
        return 0

    lax.fori_loop(0, pl.cdiv(count, PAGES), tile, 0)


def kept(array):
    return pltpu.with_memory_space_constraint(array, pltpu.VMEM)


def in_hbm(array):
    return pltpu.with_memory_space_constraint(array, pltpu.HBM)


SMEM_SPEC = pl.BlockSpec(memory_space=pltpu.SMEM)
VMEM_SPEC = pl.BlockSpec(memory_space=pltpu.VMEM)


def prompt_early(blocks, order, count, x, weights):
    rows = x.shape[0]
    n_early = 2 * len(weights)
    return pl.pallas_call(
        functools.partial(early_kernel, n_early),
        in_specs=[SMEM_SPEC] * 3
        + [pl.BlockSpec(memory_space=pl.ANY)]
        + [VMEM_SPEC] * len(weights),
        out_specs=[VMEM_SPEC] * 3,
        out_shape=[
            pltpu.VMEM((rows, WKV), F32),
            pltpu.VMEM((rows, (SECTIONS - n_early) * DEPTH), BF16),
            pltpu.VMEM((rows, 128), F32),
        ],
        scratch_shapes=[
            pltpu.VMEM((BUFFERS, TILE, D), BF16),
            pltpu.SemaphoreType.DMA((BUFFERS, PAGES)),
        ],
        compiler_params=params(24),
        name="prompt_early",
    )(blocks, order, count, x, *weights)


def late_kernel(
    order_ref, turn_ref, count_ref, cos_ref, sin_ref, acc_ref, rest_ref, squares_ref, *refs
):
    w_refs, (pages_ref, tile_ref, cos_tile, sin_tile) = refs[:-4], refs[-4:]
    count = count_ref[0]
    pages_ref[...] = jnp.zeros_like(pages_ref)

    def tile(t, _):
        rows = pl.ds(pl.multiple_of(t * TILE, TILE), TILE)
        last = count - 1 - t * PAGES
        for c in range(PAGES):
            page = turn_ref[t * PAGES + jnp.minimum(c, last)]
            turn = pl.ds(pl.multiple_of(page * PAGE, PAGE), PAGE)
            cos_tile[c * PAGE : (c + 1) * PAGE, :] = cos_ref[turn, :]
            sin_tile[c * PAGE : (c + 1) * PAGE, :] = sin_ref[turn, :]
        total = acc_ref[rows, :]
        for k, w_ref in enumerate(w_refs):
            x = rest_ref[rows, k * 2 * DEPTH : (k + 1) * 2 * DEPTH]
            total = total + jnp.dot(x, w_ref[...], preferred_element_type=F32)
        mean = jnp.sum(squares_ref[rows, :], axis=-1, keepdims=True) * (1.0 / D)
        total = total * lax.rsqrt(mean + EPS)
        tile_ref[:, :HD] = turned(total[:, :HD], cos_tile[...], sin_tile[...]).astype(BF16)
        tile_ref[:, HD:] = total[:, HD:].astype(BF16)
        for c in range(PAGES):
            source = jnp.minimum(c, last)
            slot = order_ref[t * PAGES + source]
            to = pl.ds(pl.multiple_of((slot % CAP) * PAGE, PAGE), PAGE)
            here = pl.ds(pl.multiple_of(source * PAGE, PAGE), PAGE)
            pages_ref[slot // CAP, to, :] = tile_ref[here, :]
        return 0

    lax.fori_loop(0, pl.cdiv(count, PAGES), tile, 0)


def prompt_late(order, turn, count, cosine, sine, early, weights):
    return pl.pallas_call(
        late_kernel,
        in_specs=[SMEM_SPEC] * 3 + [VMEM_SPEC] * (5 + len(weights)),
        out_specs=VMEM_SPEC,
        out_shape=jax.ShapeDtypeStruct((SECTIONS, GROUP_TOK, WKV), BF16),
        scratch_shapes=[
            pltpu.VMEM((TILE, WKV), BF16),
            pltpu.VMEM((TILE, HD), F32),
            pltpu.VMEM((TILE, HD), F32),
        ],
        compiler_params=params(16),
        name="prompt_late",
    )(order, turn, count, cosine, sine, *[kept(array) for array in early], *weights)


def project_kernel(
    slot_ref, tok_ref, gain_ref, qw_ref, kvw_ref, ids_ref, out_ref, order_ref, turn_ref, count_ref
):
    found = jnp.int32(0)
    for slot in range(SECTIONS * CAP):
        held = slot_ref[slot // CAP, slot % CAP]
        order_ref[found] = slot
        turn_ref[found] = jnp.maximum(held, 0) & (CAP - 1)
        found = found + jnp.where(held >= 0, 1, 0)
    count_ref[0] = found

    tok = tok_ref[...].astype(F32)
    scaled = (tok * gain_ref[...]).astype(BF16)
    squares = jnp.sum(tok * tok, axis=-1, keepdims=True)
    high = squares.astype(BF16).astype(F32)
    low = squares - high
    q = jnp.dot(scaled, qw_ref[...], preferred_element_type=F32)
    kv = jnp.dot(scaled, kvw_ref[...], preferred_element_type=F32)
    lane = lax.broadcasted_iota(jnp.int32, (tok.shape[0], EXTRA), 1)
    extra = jnp.where(lane == 0, high, jnp.where(lane == 1, low, 0.0))
    half = tok.shape[0] // 2
    for g in range(SECTIONS):
        ids = ids_ref[g : g + 1, :]
        for array, at, width in ((q, 0, WQ), (kv, WQ, WKV), (extra, WQ + WKV, EXTRA)):
            rows = jnp.concatenate(
                [
                    array[g * SEQ_G : (g + 1) * SEQ_G],
                    array[half + g * SEQ_G : half + (g + 1) * SEQ_G],
                ],
                axis=0,
            )
            if width == EXTRA:
                rows = rows + ids
            out_ref[g, :, at : at + width] = rows.astype(BF16)


def project(own_ids, tokens, gain, q_weight, kv_weight, ids_wide):
    slots = jax.ShapeDtypeStruct((SECTIONS * CAP,), jnp.int32)
    return pl.pallas_call(
        project_kernel,
        in_specs=[SMEM_SPEC] + [VMEM_SPEC] * 5,
        out_specs=[VMEM_SPEC] + [SMEM_SPEC] * 3,
        out_shape=[
            jax.ShapeDtypeStruct((SECTIONS, ROWS, WQ + WKV + EXTRA), BF16),
            slots,
            slots,
            jax.ShapeDtypeStruct((1,), jnp.int32),
        ],
        compiler_params=params(),
        name="project",
    )(own_ids, in_hbm(tokens), gain, in_hbm(q_weight), kv_weight, ids_wide)


def ready_kernel(ctx_ref, got_ref, cos_ref, sin_ref, q_ref, key_ref, value_ref, seq_ref):
    got = got_ref[...].astype(F32)
    total = jnp.sum(got, axis=0)
    squares = (
        total[:, WQ + WKV : WQ + WKV + 1] + total[:, WQ + WKV + 1 : WQ + WKV + 2]
    )
    rscale = lax.rsqrt(squares * (1.0 / D) + EPS)
    total = total[:, : WQ + WKV] * rscale
    cosine = jnp.concatenate(
        [cos_ref[pl.ds(ctx_ref[r % SEQ_G] + r // SEQ_G, 1), :] for r in range(ROWS)], axis=0
    )
    sine = jnp.concatenate(
        [sin_ref[pl.ds(ctx_ref[r % SEQ_G] + r // SEQ_G, 1), :] for r in range(ROWS)], axis=0
    )
    for h in range(GQ):
        q_ref[h * ROWS : (h + 1) * ROWS, :] = turned(
            total[:, h * HD : (h + 1) * HD], cosine, sine
        ).astype(BF16)
    key_ref[...] = turned(total[:, WQ : WQ + HD], cosine, sine).astype(BF16)
    value_ref[...] = total[:, WQ + HD : WQ + WKV].astype(BF16)

    ids = jnp.max(got[:, :, WQ + WKV :], axis=1)
    lane_in = lax.broadcasted_iota(jnp.int32, (EXTRA, GROUP_TOK), 0)
    lane_out = lax.broadcasted_iota(jnp.int32, (EXTRA, GROUP_TOK), 1)
    spread = (lane_in == ID_LANE + lane_out // PAGE).astype(F32)
    ids = jnp.where(
        (lax.broadcasted_iota(jnp.int32, ids.shape, 1) >= ID_LANE), ids, 0.0
    )
    ids = jnp.dot(ids, spread, preferred_element_type=F32).astype(jnp.int32)
    position = (ids & (CAP - 1)) * PAGE + (
        lax.broadcasted_iota(jnp.int32, ids.shape, 1) & (PAGE - 1)
    )
    owner = jnp.full(ids.shape, -1, jnp.int32)
    for j in range(SEQ_G):
        held = (ids >= j * CAP) & (ids < (j + 1) * CAP) & (position < ctx_ref[j])
        owner = jnp.where(held, j, owner)
    seq_ref[...] = owner


def ready(context_len, got, cosine, sine):
    vmem = pl.BlockSpec(memory_space=pltpu.VMEM)
    return pl.pallas_call(
        ready_kernel,
        in_specs=[pl.BlockSpec(memory_space=pltpu.SMEM), vmem, vmem, vmem],
        out_shape=[
            jax.ShapeDtypeStruct((GQ * ROWS, HD), BF16),
            jax.ShapeDtypeStruct((ROWS, HD), BF16),
            jax.ShapeDtypeStruct((ROWS, HD), BF16),
            jax.ShapeDtypeStruct((SECTIONS, GROUP_TOK), jnp.int32),
        ],
        compiler_params=params(),
        name="ready",
    )(context_len, got, cosine, sine)


def attend_kernel(pages_ref, q_ref, key_ref, value_ref, seq_ref, ow_ref, out_ref, ow_out, sem):
    fetch = pltpu.make_async_copy(ow_ref, ow_out, sem)
    fetch.start()
    scale = 1.0 / math.sqrt(HD)
    q = q_ref[...]
    n = GQ * ROWS

    def against(keys):
        return (
            lax.dot_general(q, keys, (((1,), (1,)), ((), ())), preferred_element_type=F32) * scale
        )

    row = lax.broadcasted_iota(jnp.int32, (n, 1), 0)
    row_seq, row_step = row & (SEQ_G - 1), (row // SEQ_G) & 1
    col = lax.broadcasted_iota(jnp.int32, (n, ROWS), 1)
    fresh_ok = ((col & (SEQ_G - 1)) == row_seq) & (col // SEQ_G <= row_step)
    fresh = jnp.where(fresh_ok, against(key_ref[...]), -jnp.inf)
    cached = []
    peak = None
    for s in range(SECTIONS):
        ok = seq_ref[s : s + 1, :] == row_seq
        scores = jnp.where(ok, against(pages_ref[s, :, :HD]), -jnp.inf)
        cached.append(scores)
        peak = scores if peak is None else jnp.maximum(peak, scores)
    highest = jnp.maximum(
        jnp.max(peak, axis=-1, keepdims=True), jnp.max(fresh, axis=-1, keepdims=True)
    )
    fresh = jnp.exp(fresh - highest)
    cached = [jnp.exp(scores - highest) for scores in cached]
    denom = cached[0]
    for scores in cached[1:]:
        denom = denom + scores
    denom = jnp.sum(denom, axis=-1, keepdims=True) + jnp.sum(fresh, axis=-1, keepdims=True)
    inverse = 1.0 / denom
    mixed = jnp.dot(
        (fresh * inverse).astype(BF16), value_ref[...], preferred_element_type=F32
    )
    for s in range(SECTIONS):
        mixed = mixed + jnp.dot(
            (cached[s] * inverse).astype(BF16), pages_ref[s, :, HD:], preferred_element_type=F32
        )
    mixed = mixed.astype(BF16)
    for d in range(SECTIONS):
        for h in range(GQ):
            out_ref[d, :, h * HD : (h + 1) * HD] = mixed[h * ROWS : (h + 1) * ROWS]
    fetch.wait()


def attend(pages, q, key, value, seq, o_weight):
    return pl.pallas_call(
        attend_kernel,
        in_specs=[VMEM_SPEC] * 5 + [pl.BlockSpec(memory_space=pl.ANY)],
        out_specs=[VMEM_SPEC] * 2,
        out_shape=[
            jax.ShapeDtypeStruct((SECTIONS, ROWS, WQ), BF16),
            pltpu.VMEM(o_weight.shape, BF16),
        ],
        scratch_shapes=[pltpu.SemaphoreType.DMA(())],
        compiler_params=params(),
        name="attend",
    )(pages, q, key, value, seq, in_hbm(o_weight))


def output_kernel(attn_ref, ow_ref, mine_ref, other_ref, total_ref):
    core = lax.axis_index("tensor") % 2
    attn = attn_ref[...].reshape(SECTIONS * ROWS, WQ)
    part = jnp.dot(attn, ow_ref[...], preferred_element_type=F32)
    total_ref[...] = part.reshape(total_ref.shape)
    for chip in range(4):
        mine_ref[chip] = total_ref[2 * chip + core]
        other_ref[chip] = total_ref[2 * chip + 1 - core].astype(BF16)


def output_part(attn, o_weight):
    width = o_weight.shape[1]
    half = (4, 2 * ROWS, width)
    return pl.pallas_call(
        output_kernel,
        out_shape=[jax.ShapeDtypeStruct(half, F32), jax.ShapeDtypeStruct(half, BF16)],
        scratch_shapes=[pltpu.VMEM((8, 2 * ROWS, width), F32)],
        compiler_params=params(),
        name="output_part",
    )(attn, kept(o_weight))


CHIP_STEPS = (1, 3, 2)


def pair_kernel(mine_ref, got_ref, own_ref, *out_refs):
    chip = lax.axis_index("tensor") // 2

    def pair(at):
        return mine_ref[at] + got_ref[at].astype(F32)

    own_ref[...] = pair(chip)
    for step, out_ref in zip(CHIP_STEPS, out_refs):
        out_ref[...] = pair((chip + step) % 4).astype(BF16)


def pair_sums(mine, got):
    piece = mine.shape[1:]
    return pl.pallas_call(
        pair_kernel,
        out_shape=[jax.ShapeDtypeStruct(piece, F32)] + [jax.ShapeDtypeStruct(piece, BF16)] * 3,
        compiler_params=params(),
        name="pair_sums",
    )(mine, got)


def finish_kernel(_, own_ref, a_ref, b_ref, c_ref, tok_ref, out_ref):
    total = own_ref[...]
    for got_ref in (a_ref, b_ref, c_ref):
        total = total + got_ref[...].astype(F32)
    tok = tok_ref[...].astype(F32)
    for i in range(2):
        rows = jnp.concatenate(
            [total[g * ROWS + i * SEQ_G : g * ROWS + (i + 1) * SEQ_G] for g in range(2)], axis=0
        )
        out_ref[i] = (tok[i] + rows).astype(BF16)


def finish(member, own, got, tokens):
    rows, width = own.shape
    block = pl.BlockSpec((2, rows // 2, width), lambda r, member: (0, member[0], 0))
    whole = pl.BlockSpec((rows, width), lambda r, member: (0, 0))
    return pl.pallas_call(
        finish_kernel,
        grid_spec=pltpu.PrefetchScalarGridSpec(
            num_scalar_prefetch=1,
            grid=(1,),
            in_specs=[whole] * 4 + [block],
            out_specs=pl.BlockSpec((2, rows // 2, width), lambda r, member: (0, 0, 0)),
        ),
        out_shape=jax.ShapeDtypeStruct((2, rows // 2, width), BF16),
        compiler_params=params(),
        name="finish",
    )(member, own, *got, tokens)


def on_device(
    prompt_rows, page_slot, context_len, new_tokens, norm_gain, q_weight, kv_weight, o_weight
):
    section = lax.axis_index("section")
    member = lax.axis_index("tensor")
    core = member % 2
    own_ids = page_slot[0]
    gain_here = lax.dynamic_slice_in_dim(norm_gain, section * DEPTH, DEPTH, 0)
    cosine, sine = rotation_tables()

    ids_wide = jnp.pad(own_ids.astype(F32), ((0, 0), (ID_LANE, EXTRA - ID_LANE - CAP)))
    payload, order, turn, count = project(
        own_ids, new_tokens.reshape(-1, DEPTH), gain_here[None, :], q_weight, kv_weight, ids_wide
    )

    weight = (kv_weight.astype(F32) * gain_here[:, None]).astype(BF16)
    from_1 = shifted(weight, 0, 1)
    from_3 = shifted(weight, 0, -1)
    from_2 = shifted(weight, 0, 2)
    near = jnp.concatenate([weight, from_1], axis=0)
    far = jnp.concatenate([from_3, from_2], axis=0)
    near, far, payload = lax.optimization_barrier((near, far, payload))
    got = lax.all_to_all(payload, "section", split_axis=0, concat_axis=0, tiled=True)
    near_p = shifted(near, 1, 1)
    far_m = shifted(far, 1, -1)
    near_2, far_2 = lax.optimization_barrier((near, far))
    far_p = shifted(far_2, 1, 1)
    near_m = shifted(near_2, 1, -1)
    near_o = shifted(near_p, 1, 1)
    far_o = shifted(far_m, 1, -1)

    def blocks(*steps):
        z, x = section // 4, section % 4
        ids = []
        for a, b in steps:
            at_0 = ((z + b) % 4) * 4 + (x + a) % 4
            at_1 = ((z + a) % 4) * 4 + (x + b) % 4
            ids.append(jnp.where(core == 0, at_0, at_1))
        return jnp.stack(ids).astype(jnp.int32)

    where = blocks(
        (0, 0), (3, 0), (1, 0), (2, 0),
        (0, 3), (3, 3), (1, 1), (2, 1),
        (0, 1), (3, 1), (1, 3), (2, 3),
        (0, 2), (3, 2), (1, 2), (2, 2),
    )
    early = prompt_early(where, order, count, prompt_rows, (near, far, near_p, far_m))
    pages = prompt_late(
        order, turn, count, cosine, sine, early, (near_m, far_p, near_o, far_o)
    )
    queries, new_keys, new_values, owners = ready(context_len, got, cosine, sine)
    received = lax.all_to_all(pages, "section", split_axis=0, concat_axis=0, tiled=True)
    attn, o_weight = attend(received, queries, new_keys, new_values, owners, o_weight)
    attn = lax.all_to_all(attn, "section", split_axis=0, concat_axis=0, tiled=True)
    mine, other = output_part(attn, o_weight)
    other = lax.ppermute(other, "tensor", [(t, t ^ 1) for t in range(8)])
    own, *pieces = pair_sums(mine, other)
    got = [
        lax.ppermute(piece, "tensor", [(t, (t + 2 * step) % 8) for t in range(8)])
        for step, piece in zip(CHIP_STEPS, pieces)
    ]
    return finish(member[None].astype(jnp.int32), own, got, new_tokens)


def solution(mesh):
    placed = (
        P("section", None),
        P("section", None, None),
        P("section"),
        P(None, None, "section"),
        P(),
        P("section", "tensor"),
        P("section", "tensor"),
        P("tensor", "section"),
    )
    return jax.shard_map(
        on_device,
        mesh=mesh,
        in_specs=placed,
        out_specs=P(None, "tensor", "section"),
        check_vma=False,
    )
```

```python
import functools
import math

import jax
import jax.numpy as jnp
from jax import lax
from jax.experimental import pallas as pl
from jax.experimental.pallas import tpu as pltpu
from jax.sharding import PartitionSpec as P

D = 8192
HD = 128
GQ = 8
PAGE = 16
CAP = 8
SEQ_G = 8
SECTIONS = 16
GROUP_TOK = CAP * PAGE
ROWS = 2 * SEQ_G
DEPTH = D // SECTIONS
WQ = GQ * HD
WKV = 2 * HD
EXTRA = 128
ID_LANE = 8
POSITIONS = 136

EPS = 1e-05
ROPE_BASE = 500000.0
BF16 = jnp.bfloat16
F32 = jnp.float32


def params(mib=16):
    return pltpu.CompilerParams(vmem_limit_bytes=mib * 1024 * 1024)


def rotation_tables():
    half = HD // 2
    frequency = ROPE_BASE ** (-2.0 * jnp.arange(half, dtype=F32) / HD)
    angles = jnp.arange(POSITIONS, dtype=jnp.int32).astype(F32)[:, None] * frequency
    cosine, sine = jnp.cos(angles), jnp.sin(angles)
    return (
        jnp.concatenate([cosine, cosine], axis=-1),
        jnp.concatenate([-sine, sine], axis=-1),
    )


def turned(rows, cosine, sine):
    return rows * cosine + pltpu.roll(rows, HD // 2, 1) * sine


def shifted(array, axis, step):
    pairs = []
    for z in range(4):
        for x in range(4):
            for member in range(8):
                along_x = (axis + member) % 2 == 0
                to_z = z if along_x else (z + step) % 4
                to_x = (x + step) % 4 if along_x else x
                pairs.append(((z * 4 + x) * 8 + member, (to_z * 4 + to_x) * 8 + member))
    return lax.ppermute(array, ("section", "tensor"), pairs)


TILE = 256
PAGES = TILE // PAGE
BUFFERS = 3


def early_kernel(n_early, blocks_ref, order_ref, count_ref, x_ref, *refs):
    w_refs, refs = refs[: n_early // 2], refs[n_early // 2 :]
    acc_ref, middle_ref, late_ref, squares_ref, buf_ref, sems = refs
    count = count_ref[0]

    def copy(t, c):
        slot = t % BUFFERS
        row = pl.multiple_of(order_ref[t * PAGES + c] * PAGE, PAGE)
        return pltpu.make_async_copy(
            x_ref.at[pl.ds(row, PAGE), :],
            buf_ref.at[slot, pl.ds(c * PAGE, PAGE), :],
            sems.at[slot, c],
        )

    def begin(t):
        for c in range(PAGES):

            @pl.when(t * PAGES + c < count)
            def _():
                copy(t, c).start()

    def end(t):
        for c in range(PAGES):

            @pl.when(t * PAGES + c < count)
            def _():
                copy(t, c).wait()

    for t in range(BUFFERS - 1):
        begin(t)

    def tile(t, _):
        begin(t + BUFFERS - 1)
        end(t)
        slot = t % BUFFERS
        rows = pl.ds(pl.multiple_of(t * TILE, TILE), TILE)

        def depth(k):
            return pl.ds(pl.multiple_of(blocks_ref[k] * DEPTH, DEPTH), DEPTH)

        total = None
        for k in range(n_early):
            w = w_refs[k // 2][(k % 2) * DEPTH : (k % 2 + 1) * DEPTH, :]
            part = jnp.dot(buf_ref[slot, :, depth(k)], w, preferred_element_type=F32)
            total = part if total is None else total + part
        acc_ref[rows, :] = total
        for k in range(n_early, SECTIONS):
            rest_ref = middle_ref if k < n_early + 4 else late_ref
            at = (k - n_early) % 4 * DEPTH
            rest_ref[rows, at : at + DEPTH] = buf_ref[slot, :, depth(k)]
        for c in range(PAGES):
            sums = [None] * 4
            for j in range(D // 128):
                piece = buf_ref[slot, c * PAGE : (c + 1) * PAGE, j * 128 : (j + 1) * 128]
                piece = piece.astype(F32)
                piece = piece * piece
                sums[j % 4] = piece if sums[j % 4] is None else sums[j % 4] + piece
            at = pl.multiple_of(t * TILE + c * PAGE, PAGE)
            squares_ref[pl.ds(at, PAGE), :] = (sums[0] + sums[1]) + (sums[2] + sums[3])
        return 0

    lax.fori_loop(0, pl.cdiv(count, PAGES), tile, 0)


def kept(array):
    return pltpu.with_memory_space_constraint(array, pltpu.VMEM)


def in_hbm(array):
    return pltpu.with_memory_space_constraint(array, pltpu.HBM)


SMEM_SPEC = pl.BlockSpec(memory_space=pltpu.SMEM)
VMEM_SPEC = pl.BlockSpec(memory_space=pltpu.VMEM)


def prompt_early(blocks, order, count, x, weights):
    rows = x.shape[0]
    n_early = 2 * len(weights)
    return pl.pallas_call(
        functools.partial(early_kernel, n_early),
        in_specs=[SMEM_SPEC] * 3
        + [pl.BlockSpec(memory_space=pl.ANY)]
        + [VMEM_SPEC] * len(weights),
        out_specs=[VMEM_SPEC] * 4,
        out_shape=[
            pltpu.VMEM((rows, WKV), F32),
            pltpu.VMEM((rows, 4 * DEPTH), BF16),
            pltpu.VMEM((rows, 4 * DEPTH), BF16),
            pltpu.VMEM((rows, 128), F32),
        ],
        scratch_shapes=[
            pltpu.VMEM((BUFFERS, TILE, D), BF16),
            pltpu.SemaphoreType.DMA((BUFFERS, PAGES)),
        ],
        compiler_params=params(24),
        name="prompt_early",
    )(blocks, order, count, x, *weights)


def middle_kernel(count_ref, acc_ref, x_ref, *refs):
    w_refs, out_ref = refs[:-1], refs[-1]

    def tile(t, _):
        rows = pl.ds(pl.multiple_of(t * TILE, TILE), TILE)
        total = acc_ref[rows, :]
        for k, w_ref in enumerate(w_refs):
            x = x_ref[rows, k * 2 * DEPTH : (k + 1) * 2 * DEPTH]
            total = total + jnp.dot(x, w_ref[...], preferred_element_type=F32)
        out_ref[rows, :] = total
        return 0

    lax.fori_loop(0, pl.cdiv(count_ref[0], PAGES), tile, 0)


def prompt_middle(count, acc, x, weights):
    return pl.pallas_call(
        middle_kernel,
        in_specs=[SMEM_SPEC] + [VMEM_SPEC] * (2 + len(weights)),
        out_specs=VMEM_SPEC,
        out_shape=pltpu.VMEM(acc.shape, F32),
        compiler_params=params(8),
        name="prompt_middle",
    )(count, kept(acc), kept(x), *weights)


def late_kernel(
    order_ref, turn_ref, count_ref, cos_ref, sin_ref, acc_ref, rest_ref, squares_ref, *refs
):
    w_refs, (pages_ref, tile_ref, cos_tile, sin_tile) = refs[:-4], refs[-4:]
    count = count_ref[0]
    pages_ref[...] = jnp.zeros_like(pages_ref)

    def tile(t, _):
        rows = pl.ds(pl.multiple_of(t * TILE, TILE), TILE)
        last = count - 1 - t * PAGES
        for c in range(PAGES):
            page = turn_ref[t * PAGES + jnp.minimum(c, last)]
            turn = pl.ds(pl.multiple_of(page * PAGE, PAGE), PAGE)
            cos_tile[c * PAGE : (c + 1) * PAGE, :] = cos_ref[turn, :]
            sin_tile[c * PAGE : (c + 1) * PAGE, :] = sin_ref[turn, :]
        total = acc_ref[rows, :]
        for k, w_ref in enumerate(w_refs):
            x = rest_ref[rows, k * 2 * DEPTH : (k + 1) * 2 * DEPTH]
            total = total + jnp.dot(x, w_ref[...], preferred_element_type=F32)
        mean = jnp.sum(squares_ref[rows, :], axis=-1, keepdims=True) * (1.0 / D)
        total = total * lax.rsqrt(mean + EPS)
        tile_ref[:, :HD] = turned(total[:, :HD], cos_tile[...], sin_tile[...]).astype(BF16)
        tile_ref[:, HD:] = total[:, HD:].astype(BF16)
        for c in range(PAGES):
            source = jnp.minimum(c, last)
            slot = order_ref[t * PAGES + source]
            to = pl.ds(pl.multiple_of((slot % CAP) * PAGE, PAGE), PAGE)
            here = pl.ds(pl.multiple_of(source * PAGE, PAGE), PAGE)
            pages_ref[slot // CAP, to, :] = tile_ref[here, :]
        return 0

    lax.fori_loop(0, pl.cdiv(count, PAGES), tile, 0)


def prompt_late(order, turn, count, cosine, sine, early, weights):
    return pl.pallas_call(
        late_kernel,
        in_specs=[SMEM_SPEC] * 3 + [VMEM_SPEC] * (5 + len(weights)),
        out_specs=VMEM_SPEC,
        out_shape=jax.ShapeDtypeStruct((SECTIONS, GROUP_TOK, WKV), BF16),
        scratch_shapes=[
            pltpu.VMEM((TILE, WKV), BF16),
            pltpu.VMEM((TILE, HD), F32),
            pltpu.VMEM((TILE, HD), F32),
        ],
        compiler_params=params(16),
        name="prompt_late",
    )(order, turn, count, cosine, sine, *[kept(array) for array in early], *weights)


def own_gain(gain_ref):
    section = lax.axis_index("section")
    return gain_ref[:, pl.ds(pl.multiple_of(section * DEPTH, DEPTH), DEPTH)]


def weight_kernel(gain_ref, kvw_ref, out_ref):
    column = jnp.broadcast_to(own_gain(gain_ref), (WKV, DEPTH)).T
    out_ref[...] = (kvw_ref[...].astype(F32) * column).astype(BF16)


def with_gain(gain, kv_weight):
    return pl.pallas_call(
        weight_kernel,
        out_shape=jax.ShapeDtypeStruct(kv_weight.shape, BF16),
        compiler_params=params(),
        name="with_gain",
    )(in_hbm(gain), in_hbm(kv_weight))


def project_kernel(
    slot_ref, tok_ref, gain_ref, qw_ref, kvw_ref, ids_ref, out_ref, order_ref, turn_ref, count_ref
):
    found = jnp.int32(0)
    for slot in range(SECTIONS * CAP):
        held = slot_ref[slot // CAP, slot % CAP]
        order_ref[found] = slot
        turn_ref[found] = jnp.maximum(held, 0) & (CAP - 1)
        found = found + jnp.where(held >= 0, 1, 0)
    count_ref[0] = found

    tok = tok_ref[...].astype(F32)
    scaled = (tok * own_gain(gain_ref)).astype(BF16)
    squares = jnp.sum(tok * tok, axis=-1, keepdims=True)
    high = squares.astype(BF16).astype(F32)
    low = squares - high
    q = jnp.dot(scaled, qw_ref[...], preferred_element_type=F32)
    kv = jnp.dot(scaled, kvw_ref[...], preferred_element_type=F32)
    lane = lax.broadcasted_iota(jnp.int32, (tok.shape[0], EXTRA), 1)
    extra = jnp.where(lane == 0, high, jnp.where(lane == 1, low, 0.0))
    half = tok.shape[0] // 2
    for g in range(SECTIONS):
        ids = ids_ref[g : g + 1, :]
        for array, at, width in ((q, 0, WQ), (kv, WQ, WKV), (extra, WQ + WKV, EXTRA)):
            rows = jnp.concatenate(
                [
                    array[g * SEQ_G : (g + 1) * SEQ_G],
                    array[half + g * SEQ_G : half + (g + 1) * SEQ_G],
                ],
                axis=0,
            )
            if width == EXTRA:
                rows = rows + ids
            out_ref[g, :, at : at + width] = rows.astype(BF16)


def project(own_ids, tokens, gain, q_weight, kv_weight, ids_wide):
    slots = jax.ShapeDtypeStruct((SECTIONS * CAP,), jnp.int32)
    return pl.pallas_call(
        project_kernel,
        in_specs=[SMEM_SPEC] + [VMEM_SPEC] * 5,
        out_specs=[VMEM_SPEC] + [SMEM_SPEC] * 3,
        out_shape=[
            jax.ShapeDtypeStruct((SECTIONS, ROWS, WQ + WKV + EXTRA), BF16),
            slots,
            slots,
            jax.ShapeDtypeStruct((1,), jnp.int32),
        ],
        compiler_params=params(),
        name="project",
    )(own_ids, in_hbm(tokens), gain, in_hbm(q_weight), kv_weight, ids_wide)


def ready_kernel(ctx_ref, got_ref, cos_ref, sin_ref, q_ref, key_ref, value_ref, seq_ref):
    got = got_ref[...].astype(F32)
    total = jnp.sum(got, axis=0)
    squares = (
        total[:, WQ + WKV : WQ + WKV + 1] + total[:, WQ + WKV + 1 : WQ + WKV + 2]
    )
    rscale = lax.rsqrt(squares * (1.0 / D) + EPS)
    total = total[:, : WQ + WKV] * rscale
    cosine = jnp.concatenate(
        [cos_ref[pl.ds(ctx_ref[r % SEQ_G] + r // SEQ_G, 1), :] for r in range(ROWS)], axis=0
    )
    sine = jnp.concatenate(
        [sin_ref[pl.ds(ctx_ref[r % SEQ_G] + r // SEQ_G, 1), :] for r in range(ROWS)], axis=0
    )
    for h in range(GQ):
        q_ref[h * ROWS : (h + 1) * ROWS, :] = turned(
            total[:, h * HD : (h + 1) * HD], cosine, sine
        ).astype(BF16)
    key_ref[...] = turned(total[:, WQ : WQ + HD], cosine, sine).astype(BF16)
    value_ref[...] = total[:, WQ + HD : WQ + WKV].astype(BF16)

    ids = jnp.max(got[:, :, WQ + WKV :], axis=1)
    lane_in = lax.broadcasted_iota(jnp.int32, (EXTRA, GROUP_TOK), 0)
    lane_out = lax.broadcasted_iota(jnp.int32, (EXTRA, GROUP_TOK), 1)
    spread = (lane_in == ID_LANE + lane_out // PAGE).astype(F32)
    ids = jnp.where(
        (lax.broadcasted_iota(jnp.int32, ids.shape, 1) >= ID_LANE), ids, 0.0
    )
    ids = jnp.dot(ids, spread, preferred_element_type=F32).astype(jnp.int32)
    position = (ids & (CAP - 1)) * PAGE + (
        lax.broadcasted_iota(jnp.int32, ids.shape, 1) & (PAGE - 1)
    )
    owner = jnp.full(ids.shape, -1, jnp.int32)
    for j in range(SEQ_G):
        held = (ids >= j * CAP) & (ids < (j + 1) * CAP) & (position < ctx_ref[j])
        owner = jnp.where(held, j, owner)
    seq_ref[...] = owner


def ready(context_len, got, cosine, sine):
    vmem = pl.BlockSpec(memory_space=pltpu.VMEM)
    return pl.pallas_call(
        ready_kernel,
        in_specs=[pl.BlockSpec(memory_space=pltpu.SMEM), vmem, vmem, vmem],
        out_shape=[
            jax.ShapeDtypeStruct((GQ * ROWS, HD), BF16),
            jax.ShapeDtypeStruct((ROWS, HD), BF16),
            jax.ShapeDtypeStruct((ROWS, HD), BF16),
            jax.ShapeDtypeStruct((SECTIONS, GROUP_TOK), jnp.int32),
        ],
        compiler_params=params(),
        name="ready",
    )(context_len, got, cosine, sine)


def attend_kernel(pages_ref, q_ref, key_ref, value_ref, seq_ref, ow_ref, out_ref, ow_out, sem):
    fetch = pltpu.make_async_copy(ow_ref, ow_out, sem)
    fetch.start()
    scale = 1.0 / math.sqrt(HD)
    q = q_ref[...]
    n = GQ * ROWS

    def against(keys):
        return (
            lax.dot_general(q, keys, (((1,), (1,)), ((), ())), preferred_element_type=F32) * scale
        )

    row = lax.broadcasted_iota(jnp.int32, (n, 1), 0)
    row_seq, row_step = row & (SEQ_G - 1), (row // SEQ_G) & 1
    col = lax.broadcasted_iota(jnp.int32, (n, ROWS), 1)
    fresh_ok = ((col & (SEQ_G - 1)) == row_seq) & (col // SEQ_G <= row_step)
    fresh = jnp.where(fresh_ok, against(key_ref[...]), -jnp.inf)
    cached = []
    peak = None
    for s in range(SECTIONS):
        ok = seq_ref[s : s + 1, :] == row_seq
        scores = jnp.where(ok, against(pages_ref[s, :, :HD]), -jnp.inf)
        cached.append(scores)
        peak = scores if peak is None else jnp.maximum(peak, scores)
    highest = jnp.maximum(
        jnp.max(peak, axis=-1, keepdims=True), jnp.max(fresh, axis=-1, keepdims=True)
    )
    fresh = jnp.exp(fresh - highest)
    cached = [jnp.exp(scores - highest) for scores in cached]
    denom = cached[0]
    for scores in cached[1:]:
        denom = denom + scores
    denom = jnp.sum(denom, axis=-1, keepdims=True) + jnp.sum(fresh, axis=-1, keepdims=True)
    inverse = 1.0 / denom
    mixed = jnp.dot(
        (fresh * inverse).astype(BF16), value_ref[...], preferred_element_type=F32
    )
    for s in range(SECTIONS):
        mixed = mixed + jnp.dot(
            (cached[s] * inverse).astype(BF16), pages_ref[s, :, HD:], preferred_element_type=F32
        )
    mixed = mixed.astype(BF16)
    for d in range(SECTIONS):
        for h in range(GQ):
            out_ref[d, :, h * HD : (h + 1) * HD] = mixed[h * ROWS : (h + 1) * ROWS]
    fetch.wait()


def attend(pages, q, key, value, seq, o_weight):
    return pl.pallas_call(
        attend_kernel,
        in_specs=[VMEM_SPEC] * 5 + [pl.BlockSpec(memory_space=pl.ANY)],
        out_specs=[VMEM_SPEC] * 2,
        out_shape=[
            jax.ShapeDtypeStruct((SECTIONS, ROWS, WQ), BF16),
            pltpu.VMEM(o_weight.shape, BF16),
        ],
        scratch_shapes=[pltpu.SemaphoreType.DMA(())],
        compiler_params=params(),
        name="attend",
    )(pages, q, key, value, seq, in_hbm(o_weight))


def output_kernel(attn_ref, ow_ref, mine_ref, other_ref, total_ref):
    core = lax.axis_index("tensor") % 2
    attn = attn_ref[...].reshape(SECTIONS * ROWS, WQ)
    part = jnp.dot(attn, ow_ref[...], preferred_element_type=F32)
    total_ref[...] = part.reshape(total_ref.shape)
    for chip in range(4):
        mine_ref[chip] = total_ref[2 * chip + core]
        other_ref[chip] = total_ref[2 * chip + 1 - core].astype(BF16)


def output_part(attn, o_weight):
    width = o_weight.shape[1]
    half = (4, 2 * ROWS, width)
    return pl.pallas_call(
        output_kernel,
        out_shape=[jax.ShapeDtypeStruct(half, F32), jax.ShapeDtypeStruct(half, BF16)],
        scratch_shapes=[pltpu.VMEM((8, 2 * ROWS, width), F32)],
        compiler_params=params(),
        name="output_part",
    )(attn, kept(o_weight))


CHIP_STEPS = (1, 3, 2)


def pair_kernel(mine_ref, got_ref, own_ref, *out_refs):
    chip = lax.axis_index("tensor") // 2

    def pair(at):
        return mine_ref[at] + got_ref[at].astype(F32)

    own_ref[...] = pair(chip)
    for step, out_ref in zip(CHIP_STEPS, out_refs):
        out_ref[...] = pair((chip + step) % 4).astype(BF16)


def pair_sums(mine, got):
    piece = mine.shape[1:]
    return pl.pallas_call(
        pair_kernel,
        out_shape=[jax.ShapeDtypeStruct(piece, F32)] + [jax.ShapeDtypeStruct(piece, BF16)] * 3,
        compiler_params=params(),
        name="pair_sums",
    )(mine, got)


def finish_kernel(_, own_ref, a_ref, b_ref, c_ref, tok_ref, out_ref):
    total = own_ref[...]
    for got_ref in (a_ref, b_ref, c_ref):
        total = total + got_ref[...].astype(F32)
    tok = tok_ref[...].astype(F32)
    for i in range(2):
        rows = jnp.concatenate(
            [total[g * ROWS + i * SEQ_G : g * ROWS + (i + 1) * SEQ_G] for g in range(2)], axis=0
        )
        out_ref[i] = (tok[i] + rows).astype(BF16)


def finish(member, own, got, tokens):
    rows, width = own.shape
    block = pl.BlockSpec((2, rows // 2, width), lambda r, member: (0, member[0], 0))
    whole = pl.BlockSpec((rows, width), lambda r, member: (0, 0))
    return pl.pallas_call(
        finish_kernel,
        grid_spec=pltpu.PrefetchScalarGridSpec(
            num_scalar_prefetch=1,
            grid=(1,),
            in_specs=[whole] * 4 + [block],
            out_specs=pl.BlockSpec((2, rows // 2, width), lambda r, member: (0, 0, 0)),
        ),
        out_shape=jax.ShapeDtypeStruct((2, rows // 2, width), BF16),
        compiler_params=params(),
        name="finish",
    )(member, own, *got, tokens)


def on_device(
    prompt_rows, page_slot, context_len, new_tokens, norm_gain, q_weight, kv_weight, o_weight
):
    section = lax.axis_index("section")
    member = lax.axis_index("tensor")
    core = member % 2
    own_ids = page_slot[0]
    cosine, sine = rotation_tables()

    ids_wide = jnp.pad(own_ids.astype(F32), ((0, 0), (ID_LANE, EXTRA - ID_LANE - CAP)))
    payload, order, turn, count = project(
        own_ids, new_tokens.reshape(-1, DEPTH), norm_gain[None, :], q_weight, kv_weight, ids_wide
    )

    weight = with_gain(norm_gain[None, :], kv_weight)
    from_1 = shifted(weight, 0, 1)
    from_3 = shifted(weight, 0, -1)
    from_2 = shifted(weight, 0, 2)
    near = jnp.concatenate([weight, from_1], axis=0)
    far = jnp.concatenate([from_3, from_2], axis=0)
    near, far, payload = lax.optimization_barrier((near, far, payload))
    got = lax.all_to_all(payload, "section", split_axis=0, concat_axis=0, tiled=True)
    near_p = shifted(near, 1, 1)
    far_m = shifted(far, 1, -1)
    near_2, far_2 = lax.optimization_barrier((near, far))
    far_p = shifted(far_2, 1, 1)
    near_m = shifted(near_2, 1, -1)
    near_o = shifted(near_p, 1, 1)
    far_o = shifted(far_m, 1, -1)

    def blocks(*steps):
        z, x = section // 4, section % 4
        ids = []
        for a, b in steps:
            at_0 = ((z + b) % 4) * 4 + (x + a) % 4
            at_1 = ((z + a) % 4) * 4 + (x + b) % 4
            ids.append(jnp.where(core == 0, at_0, at_1))
        return jnp.stack(ids).astype(jnp.int32)

    where = blocks(
        (0, 0), (3, 0), (1, 0), (2, 0),
        (0, 3), (3, 3), (1, 1), (2, 1),
        (0, 1), (3, 1), (1, 3), (2, 3),
        (0, 2), (3, 2), (1, 2), (2, 2),
    )
    acc, x_middle, x_late, squares = prompt_early(
        where, order, count, prompt_rows, (near, far, near_p, far_m)
    )
    acc = prompt_middle(count, acc, x_middle, (near_m, far_p))
    pages = prompt_late(
        order, turn, count, cosine, sine, (acc, x_late, squares), (near_o, far_o)
    )
    queries, new_keys, new_values, owners = ready(context_len, got, cosine, sine)
    received = lax.all_to_all(pages, "section", split_axis=0, concat_axis=0, tiled=True)
    attn, o_weight = attend(received, queries, new_keys, new_values, owners, o_weight)
    attn = lax.all_to_all(attn, "section", split_axis=0, concat_axis=0, tiled=True)
    mine, other = output_part(attn, o_weight)
    other = lax.ppermute(other, "tensor", [(t, t ^ 1) for t in range(8)])
    own, *pieces = pair_sums(mine, other)
    got = [
        lax.ppermute(piece, "tensor", [(t, (t + 2 * step) % 8) for t in range(8)])
        for step, piece in zip(CHIP_STEPS, pieces)
    ]
    return finish(member[None].astype(jnp.int32), own, got, new_tokens)


def solution(mesh):
    placed = (
        P("section", None),
        P("section", None, None),
        P("section"),
        P(None, None, "section"),
        P(),
        P("section", "tensor"),
        P("section", "tensor"),
        P("tensor", "section"),
    )
    return jax.shard_map(
        on_device,
        mesh=mesh,
        in_specs=placed,
        out_specs=P(None, "tensor", "section"),
        check_vma=False,
    )
```

```python
import functools
import math

import jax
import jax.numpy as jnp
from jax import lax
from jax.experimental import pallas as pl
from jax.experimental.pallas import tpu as pltpu
from jax.sharding import PartitionSpec as P

D = 8192
HD = 128
GQ = 8
PAGE = 16
CAP = 8
SEQ_G = 8
SECTIONS = 16
GROUP_TOK = CAP * PAGE
ROWS = 2 * SEQ_G
DEPTH = D // SECTIONS
WQ = GQ * HD
WKV = 2 * HD
EXTRA = 128
ID_LANE = 8
POSITIONS = 136

EPS = 1e-05
ROPE_BASE = 500000.0
BF16 = jnp.bfloat16
F32 = jnp.float32


def params(mib=16):
    return pltpu.CompilerParams(vmem_limit_bytes=mib * 1024 * 1024)


def rotation_tables():
    half = HD // 2
    frequency = ROPE_BASE ** (-2.0 * jnp.arange(half, dtype=F32) / HD)
    angles = jnp.arange(POSITIONS, dtype=jnp.int32).astype(F32)[:, None] * frequency
    cosine, sine = jnp.cos(angles), jnp.sin(angles)
    return (
        jnp.concatenate([cosine, cosine], axis=-1),
        jnp.concatenate([-sine, sine], axis=-1),
    )


def turned(rows, cosine, sine):
    return rows * cosine + pltpu.roll(rows, HD // 2, 1) * sine


def shifted(array, axis, step):
    pairs = []
    for z in range(4):
        for x in range(4):
            for member in range(8):
                along_x = (axis + member) % 2 == 0
                to_z = z if along_x else (z + step) % 4
                to_x = (x + step) % 4 if along_x else x
                pairs.append(((z * 4 + x) * 8 + member, (to_z * 4 + to_x) * 8 + member))
    return lax.ppermute(array, ("section", "tensor"), pairs)


TILE = 256
PAGES = TILE // PAGE
EARLY_TILE = 128
EARLY_PAGES = EARLY_TILE // PAGE
BUFFERS = 6


def early_kernel(n_early, blocks_ref, order_ref, count_ref, x_ref, *refs):
    w_refs, refs = refs[: n_early // 2], refs[n_early // 2 :]
    acc_ref, middle_ref, late_ref, squares_ref, buf_ref, sems = refs
    count = count_ref[0]

    def copy(t, c):
        slot = t % BUFFERS
        row = pl.multiple_of(order_ref[t * EARLY_PAGES + c] * PAGE, PAGE)
        return pltpu.make_async_copy(
            x_ref.at[pl.ds(row, PAGE), :],
            buf_ref.at[slot, pl.ds(c * PAGE, PAGE), :],
            sems.at[slot, c],
        )

    def begin(t):
        for c in range(EARLY_PAGES):

            @pl.when(t * EARLY_PAGES + c < count)
            def _():
                copy(t, c).start()

    def end(t):
        for c in range(EARLY_PAGES):

            @pl.when(t * EARLY_PAGES + c < count)
            def _():
                copy(t, c).wait()

    for t in range(BUFFERS - 1):
        begin(t)

    def tile(t, _):
        begin(t + BUFFERS - 1)
        end(t)
        slot = t % BUFFERS
        rows = pl.ds(pl.multiple_of(t * EARLY_TILE, EARLY_TILE), EARLY_TILE)

        def depth(k):
            return pl.ds(pl.multiple_of(blocks_ref[k] * DEPTH, DEPTH), DEPTH)

        total = None
        for k in range(n_early):
            w = w_refs[k // 2][(k % 2) * DEPTH : (k % 2 + 1) * DEPTH, :]
            part = jnp.dot(buf_ref[slot, :, depth(k)], w, preferred_element_type=F32)
            total = part if total is None else total + part
        acc_ref[rows, :] = total
        for c in range(EARLY_PAGES):
            at = pl.ds(pl.multiple_of(t * EARLY_TILE + c * PAGE, PAGE), PAGE)
            sums = [None] * (DEPTH // 128)
            for k in range(SECTIONS):
                block = buf_ref[slot, c * PAGE : (c + 1) * PAGE, depth(k)]
                if k >= n_early:
                    rest_ref = middle_ref if k < n_early + 4 else late_ref
                    to = (k - n_early) % 4 * DEPTH
                    rest_ref[at, to : to + DEPTH] = block
                for j in range(len(sums)):
                    piece = block[:, j * 128 : (j + 1) * 128].astype(F32)
                    piece = piece * piece
                    sums[j] = piece if sums[j] is None else sums[j] + piece
            squares_ref[at, :] = (sums[0] + sums[1]) + (sums[2] + sums[3])
        return 0

    lax.fori_loop(0, pl.cdiv(count, EARLY_PAGES), tile, 0)


def kept(array):
    return pltpu.with_memory_space_constraint(array, pltpu.VMEM)


def in_hbm(array):
    return pltpu.with_memory_space_constraint(array, pltpu.HBM)


SMEM_SPEC = pl.BlockSpec(memory_space=pltpu.SMEM)
VMEM_SPEC = pl.BlockSpec(memory_space=pltpu.VMEM)


def prompt_early(blocks, order, count, x, weights):
    rows = x.shape[0]
    n_early = 2 * len(weights)
    return pl.pallas_call(
        functools.partial(early_kernel, n_early),
        in_specs=[SMEM_SPEC] * 3
        + [pl.BlockSpec(memory_space=pl.ANY)]
        + [VMEM_SPEC] * len(weights),
        out_specs=[VMEM_SPEC] * 4,
        out_shape=[
            pltpu.VMEM((rows, WKV), F32),
            pltpu.VMEM((rows, 4 * DEPTH), BF16),
            pltpu.VMEM((rows, 4 * DEPTH), BF16),
            pltpu.VMEM((rows, 128), F32),
        ],
        scratch_shapes=[
            pltpu.VMEM((BUFFERS, EARLY_TILE, D), BF16),
            pltpu.SemaphoreType.DMA((BUFFERS, EARLY_PAGES)),
        ],
        compiler_params=params(24),
        name="prompt_early",
    )(blocks, order, count, x, *weights)


def middle_kernel(count_ref, acc_ref, x_ref, *refs):
    w_refs, out_ref = refs[:-1], refs[-1]

    def tile(t, _):
        rows = pl.ds(pl.multiple_of(t * TILE, TILE), TILE)
        total = acc_ref[rows, :]
        for k, w_ref in enumerate(w_refs):
            x = x_ref[rows, k * 2 * DEPTH : (k + 1) * 2 * DEPTH]
            total = total + jnp.dot(x, w_ref[...], preferred_element_type=F32)
        out_ref[rows, :] = total
        return 0

    lax.fori_loop(0, pl.cdiv(count_ref[0], PAGES), tile, 0)


def prompt_middle(count, acc, x, weights):
    return pl.pallas_call(
        middle_kernel,
        in_specs=[SMEM_SPEC] + [VMEM_SPEC] * (2 + len(weights)),
        out_specs=VMEM_SPEC,
        out_shape=pltpu.VMEM(acc.shape, F32),
        compiler_params=params(8),
        name="prompt_middle",
    )(count, kept(acc), kept(x), *weights)


def late_kernel(
    order_ref, turn_ref, count_ref, cos_ref, sin_ref, acc_ref, rest_ref, squares_ref, *refs
):
    w_refs, pages_ref = refs[:-1], refs[-1]
    count = count_ref[0]
    pages_ref[...] = jnp.zeros_like(pages_ref)

    def tile(t, _):
        rows = pl.ds(pl.multiple_of(t * TILE, TILE), TILE)
        last = count - 1 - t * PAGES
        total = acc_ref[rows, :]
        for k, w_ref in enumerate(w_refs):
            x = rest_ref[rows, k * 2 * DEPTH : (k + 1) * 2 * DEPTH]
            total = total + jnp.dot(x, w_ref[...], preferred_element_type=F32)
        mean = jnp.sum(squares_ref[rows, :], axis=-1, keepdims=True) * (1.0 / D)
        total = total * lax.rsqrt(mean + EPS)
        for c in reversed(range(PAGES)):
            at = t * PAGES + jnp.minimum(c, last)
            turn = pl.ds(pl.multiple_of(turn_ref[at] * PAGE, PAGE), PAGE)
            slot = order_ref[at]
            to = pl.ds(pl.multiple_of((slot & (CAP - 1)) * PAGE, PAGE), PAGE)
            here = total[c * PAGE : (c + 1) * PAGE]
            key = turned(here[:, :HD], cos_ref[turn, :], sin_ref[turn, :])
            pages_ref[slot // CAP, to, :HD] = key.astype(BF16)
            pages_ref[slot // CAP, to, HD:] = here[:, HD:].astype(BF16)
        return 0

    lax.fori_loop(0, pl.cdiv(count, PAGES), tile, 0)


def prompt_late(order, turn, count, cosine, sine, early, weights):
    return pl.pallas_call(
        late_kernel,
        in_specs=[SMEM_SPEC] * 3 + [VMEM_SPEC] * (5 + len(weights)),
        out_specs=VMEM_SPEC,
        out_shape=jax.ShapeDtypeStruct((SECTIONS, GROUP_TOK, WKV), BF16),
        compiler_params=params(16),
        name="prompt_late",
    )(order, turn, count, cosine, sine, *[kept(array) for array in early], *weights)


def own_gain(gain_ref):
    section = lax.axis_index("section")
    return gain_ref[:, pl.ds(pl.multiple_of(section * DEPTH, DEPTH), DEPTH)]


def weight_kernel(gain_ref, kvw_ref, out_ref):
    column = jnp.broadcast_to(own_gain(gain_ref), (WKV, DEPTH)).T
    out_ref[...] = (kvw_ref[...].astype(F32) * column).astype(BF16)


def with_gain(gain, kv_weight):
    return pl.pallas_call(
        weight_kernel,
        out_shape=jax.ShapeDtypeStruct(kv_weight.shape, BF16),
        compiler_params=params(),
        name="with_gain",
    )(in_hbm(gain), in_hbm(kv_weight))


def project_kernel(
    slot_ref, tok_ref, gain_ref, qw_ref, kvw_ref, ids_ref, out_ref, order_ref, turn_ref, count_ref
):
    found = jnp.int32(0)
    for slot in range(SECTIONS * CAP):
        held = slot_ref[slot // CAP, slot % CAP]
        order_ref[found] = slot
        turn_ref[found] = jnp.maximum(held, 0) & (CAP - 1)
        found = found + jnp.where(held >= 0, 1, 0)
    count_ref[0] = found

    tok = tok_ref[...].astype(F32)
    scaled = (tok * own_gain(gain_ref)).astype(BF16)
    squares = jnp.sum(tok * tok, axis=-1, keepdims=True)
    high = squares.astype(BF16).astype(F32)
    low = squares - high
    q = jnp.dot(scaled, qw_ref[...], preferred_element_type=F32)
    kv = jnp.dot(scaled, kvw_ref[...], preferred_element_type=F32)
    lane = lax.broadcasted_iota(jnp.int32, (tok.shape[0], EXTRA), 1)
    extra = jnp.where(lane == 0, high, jnp.where(lane == 1, low, 0.0))
    half = tok.shape[0] // 2
    for g in range(SECTIONS):
        ids = ids_ref[g : g + 1, :]
        for array, at, width in ((q, 0, WQ), (kv, WQ, WKV), (extra, WQ + WKV, EXTRA)):
            rows = jnp.concatenate(
                [
                    array[g * SEQ_G : (g + 1) * SEQ_G],
                    array[half + g * SEQ_G : half + (g + 1) * SEQ_G],
                ],
                axis=0,
            )
            if width == EXTRA:
                rows = rows + ids
            out_ref[g, :, at : at + width] = rows.astype(BF16)


def project(own_ids, tokens, gain, q_weight, kv_weight, ids_wide):
    slots = jax.ShapeDtypeStruct((SECTIONS * CAP,), jnp.int32)
    return pl.pallas_call(
        project_kernel,
        in_specs=[SMEM_SPEC] + [VMEM_SPEC] * 5,
        out_specs=[VMEM_SPEC] + [SMEM_SPEC] * 3,
        out_shape=[
            jax.ShapeDtypeStruct((SECTIONS, ROWS, WQ + WKV + EXTRA), BF16),
            slots,
            slots,
            jax.ShapeDtypeStruct((1,), jnp.int32),
        ],
        compiler_params=params(),
        name="project",
    )(own_ids, in_hbm(tokens), gain, in_hbm(q_weight), kv_weight, ids_wide)


def ready_kernel(ctx_ref, got_ref, cos_ref, sin_ref, q_ref, key_ref, value_ref, seq_ref):
    got = got_ref[...].astype(F32)
    total = jnp.sum(got, axis=0)
    squares = (
        total[:, WQ + WKV : WQ + WKV + 1] + total[:, WQ + WKV + 1 : WQ + WKV + 2]
    )
    rscale = lax.rsqrt(squares * (1.0 / D) + EPS)
    total = total[:, : WQ + WKV] * rscale
    cosine = jnp.concatenate(
        [cos_ref[pl.ds(ctx_ref[r % SEQ_G] + r // SEQ_G, 1), :] for r in range(ROWS)], axis=0
    )
    sine = jnp.concatenate(
        [sin_ref[pl.ds(ctx_ref[r % SEQ_G] + r // SEQ_G, 1), :] for r in range(ROWS)], axis=0
    )
    for h in range(GQ):
        q_ref[h * ROWS : (h + 1) * ROWS, :] = turned(
            total[:, h * HD : (h + 1) * HD], cosine, sine
        ).astype(BF16)
    key_ref[...] = turned(total[:, WQ : WQ + HD], cosine, sine).astype(BF16)
    value_ref[...] = total[:, WQ + HD : WQ + WKV].astype(BF16)

    ids = jnp.max(got[:, :, WQ + WKV :], axis=1)
    lane_in = lax.broadcasted_iota(jnp.int32, (EXTRA, GROUP_TOK), 0)
    lane_out = lax.broadcasted_iota(jnp.int32, (EXTRA, GROUP_TOK), 1)
    spread = (lane_in == ID_LANE + lane_out // PAGE).astype(F32)
    ids = jnp.where(
        (lax.broadcasted_iota(jnp.int32, ids.shape, 1) >= ID_LANE), ids, 0.0
    )
    ids = jnp.dot(ids, spread, preferred_element_type=F32).astype(jnp.int32)
    position = (ids & (CAP - 1)) * PAGE + (
        lax.broadcasted_iota(jnp.int32, ids.shape, 1) & (PAGE - 1)
    )
    owner = jnp.full(ids.shape, -1, jnp.int32)
    for j in range(SEQ_G):
        held = (ids >= j * CAP) & (ids < (j + 1) * CAP) & (position < ctx_ref[j])
        owner = jnp.where(held, j, owner)
    seq_ref[...] = owner


def ready(context_len, got, cosine, sine):
    vmem = pl.BlockSpec(memory_space=pltpu.VMEM)
    return pl.pallas_call(
        ready_kernel,
        in_specs=[pl.BlockSpec(memory_space=pltpu.SMEM), vmem, vmem, vmem],
        out_shape=[
            jax.ShapeDtypeStruct((GQ * ROWS, HD), BF16),
            jax.ShapeDtypeStruct((ROWS, HD), BF16),
            jax.ShapeDtypeStruct((ROWS, HD), BF16),
            jax.ShapeDtypeStruct((SECTIONS, GROUP_TOK), jnp.int32),
        ],
        compiler_params=params(),
        name="ready",
    )(context_len, got, cosine, sine)


def attend_kernel(pages_ref, q_ref, key_ref, value_ref, seq_ref, ow_ref, out_ref, ow_out, sem):
    fetch = pltpu.make_async_copy(ow_ref, ow_out, sem)
    fetch.start()
    scale = 1.0 / math.sqrt(HD)
    q = q_ref[...]
    n = GQ * ROWS

    def against(keys):
        return (
            lax.dot_general(q, keys, (((1,), (1,)), ((), ())), preferred_element_type=F32) * scale
        )

    row = lax.broadcasted_iota(jnp.int32, (n, 1), 0)
    row_seq, row_step = row & (SEQ_G - 1), (row // SEQ_G) & 1
    col = lax.broadcasted_iota(jnp.int32, (n, ROWS), 1)
    fresh_ok = ((col & (SEQ_G - 1)) == row_seq) & (col // SEQ_G <= row_step)
    fresh = jnp.where(fresh_ok, against(key_ref[...]), -jnp.inf)
    cached = []
    peak = None
    for s in range(SECTIONS):
        ok = seq_ref[s : s + 1, :] == row_seq
        scores = jnp.where(ok, against(pages_ref[s, :, :HD]), -jnp.inf)
        cached.append(scores)
        peak = scores if peak is None else jnp.maximum(peak, scores)
    highest = jnp.maximum(
        jnp.max(peak, axis=-1, keepdims=True), jnp.max(fresh, axis=-1, keepdims=True)
    )
    fresh = jnp.exp(fresh - highest)
    cached = [jnp.exp(scores - highest) for scores in cached]
    denom = cached[0]
    for scores in cached[1:]:
        denom = denom + scores
    denom = jnp.sum(denom, axis=-1, keepdims=True) + jnp.sum(fresh, axis=-1, keepdims=True)
    inverse = 1.0 / denom
    mixed = jnp.dot(
        (fresh * inverse).astype(BF16), value_ref[...], preferred_element_type=F32
    )
    for s in range(SECTIONS):
        mixed = mixed + jnp.dot(
            (cached[s] * inverse).astype(BF16), pages_ref[s, :, HD:], preferred_element_type=F32
        )
    mixed = mixed.astype(BF16)
    for d in range(SECTIONS):
        for h in range(GQ):
            out_ref[d, :, h * HD : (h + 1) * HD] = mixed[h * ROWS : (h + 1) * ROWS]
    fetch.wait()


def attend(pages, q, key, value, seq, o_weight):
    return pl.pallas_call(
        attend_kernel,
        in_specs=[VMEM_SPEC] * 5 + [pl.BlockSpec(memory_space=pl.ANY)],
        out_specs=[VMEM_SPEC] * 2,
        out_shape=[
            jax.ShapeDtypeStruct((SECTIONS, ROWS, WQ), BF16),
            pltpu.VMEM(o_weight.shape, BF16),
        ],
        scratch_shapes=[pltpu.SemaphoreType.DMA(())],
        compiler_params=params(),
        name="attend",
    )(pages, q, key, value, seq, in_hbm(o_weight))


def output_kernel(attn_ref, ow_ref, mine_ref, other_ref, total_ref):
    core = lax.axis_index("tensor") % 2
    attn = attn_ref[...].reshape(SECTIONS * ROWS, WQ)
    part = jnp.dot(attn, ow_ref[...], preferred_element_type=F32)
    total_ref[...] = part.reshape(total_ref.shape)
    for chip in range(4):
        mine_ref[chip] = total_ref[2 * chip + core]
        other_ref[chip] = total_ref[2 * chip + 1 - core].astype(BF16)


def output_part(attn, o_weight):
    width = o_weight.shape[1]
    half = (4, 2 * ROWS, width)
    return pl.pallas_call(
        output_kernel,
        out_shape=[jax.ShapeDtypeStruct(half, F32), jax.ShapeDtypeStruct(half, BF16)],
        scratch_shapes=[pltpu.VMEM((8, 2 * ROWS, width), F32)],
        compiler_params=params(),
        name="output_part",
    )(attn, kept(o_weight))


CHIP_STEPS = (1, 3, 2)


def pair_kernel(mine_ref, got_ref, own_ref, *out_refs):
    chip = lax.axis_index("tensor") // 2

    def pair(at):
        return mine_ref[at] + got_ref[at].astype(F32)

    own_ref[...] = pair(chip)
    for step, out_ref in zip(CHIP_STEPS, out_refs):
        out_ref[...] = pair((chip + step) % 4).astype(BF16)


def pair_sums(mine, got):
    piece = mine.shape[1:]
    return pl.pallas_call(
        pair_kernel,
        out_shape=[jax.ShapeDtypeStruct(piece, F32)] + [jax.ShapeDtypeStruct(piece, BF16)] * 3,
        compiler_params=params(),
        name="pair_sums",
    )(mine, got)


def finish_kernel(_, own_ref, a_ref, b_ref, c_ref, tok_ref, out_ref):
    total = own_ref[...]
    for got_ref in (a_ref, b_ref, c_ref):
        total = total + got_ref[...].astype(F32)
    tok = tok_ref[...].astype(F32)
    for i in range(2):
        rows = jnp.concatenate(
            [total[g * ROWS + i * SEQ_G : g * ROWS + (i + 1) * SEQ_G] for g in range(2)], axis=0
        )
        out_ref[i] = (tok[i] + rows).astype(BF16)


def finish(member, own, got, tokens):
    rows, width = own.shape
    block = pl.BlockSpec((2, rows // 2, width), lambda r, member: (0, member[0], 0))
    whole = pl.BlockSpec((rows, width), lambda r, member: (0, 0))
    return pl.pallas_call(
        finish_kernel,
        grid_spec=pltpu.PrefetchScalarGridSpec(
            num_scalar_prefetch=1,
            grid=(1,),
            in_specs=[whole] * 4 + [block],
            out_specs=pl.BlockSpec((2, rows // 2, width), lambda r, member: (0, 0, 0)),
        ),
        out_shape=jax.ShapeDtypeStruct((2, rows // 2, width), BF16),
        compiler_params=params(),
        name="finish",
    )(member, own, *got, tokens)


def on_device(
    prompt_rows, page_slot, context_len, new_tokens, norm_gain, q_weight, kv_weight, o_weight
):
    section = lax.axis_index("section")
    member = lax.axis_index("tensor")
    core = member % 2
    own_ids = page_slot[0]
    cosine, sine = rotation_tables()

    ids_wide = jnp.pad(own_ids.astype(F32), ((0, 0), (ID_LANE, EXTRA - ID_LANE - CAP)))
    payload, order, turn, count = project(
        own_ids, new_tokens.reshape(-1, DEPTH), norm_gain[None, :], q_weight, kv_weight, ids_wide
    )

    weight = with_gain(norm_gain[None, :], kv_weight)
    from_1 = shifted(weight, 0, 1)
    from_3 = shifted(weight, 0, -1)
    from_2 = shifted(weight, 0, 2)
    near = jnp.concatenate([weight, from_1], axis=0)
    far = jnp.concatenate([from_3, from_2], axis=0)
    near, far, payload = lax.optimization_barrier((near, far, payload))
    got = lax.all_to_all(payload, "section", split_axis=0, concat_axis=0, tiled=True)
    near_p = shifted(near, 1, 1)
    far_m = shifted(far, 1, -1)
    near_2, far_2 = lax.optimization_barrier((near, far))
    far_p = shifted(far_2, 1, 1)
    near_m = shifted(near_2, 1, -1)
    near_o = shifted(near_p, 1, 1)
    far_o = shifted(far_m, 1, -1)

    def blocks(*steps):
        z, x = section // 4, section % 4
        ids = []
        for a, b in steps:
            at_0 = ((z + b) % 4) * 4 + (x + a) % 4
            at_1 = ((z + a) % 4) * 4 + (x + b) % 4
            ids.append(jnp.where(core == 0, at_0, at_1))
        return jnp.stack(ids).astype(jnp.int32)

    where = blocks(
        (0, 0), (3, 0), (1, 0), (2, 0),
        (0, 3), (3, 3), (1, 1), (2, 1),
        (0, 1), (3, 1), (1, 3), (2, 3),
        (0, 2), (3, 2), (1, 2), (2, 2),
    )
    acc, x_middle, x_late, squares = prompt_early(
        where, order, count, prompt_rows, (near, far, near_p, far_m)
    )
    acc = prompt_middle(count, acc, x_middle, (near_m, far_p))
    pages = prompt_late(
        order, turn, count, cosine, sine, (acc, x_late, squares), (near_o, far_o)
    )
    queries, new_keys, new_values, owners = ready(context_len, got, cosine, sine)
    received = lax.all_to_all(pages, "section", split_axis=0, concat_axis=0, tiled=True)
    attn, o_weight = attend(received, queries, new_keys, new_values, owners, o_weight)
    attn = lax.all_to_all(attn, "section", split_axis=0, concat_axis=0, tiled=True)
    mine, other = output_part(attn, o_weight)
    other = lax.ppermute(other, "tensor", [(t, t ^ 1) for t in range(8)])
    own, *pieces = pair_sums(mine, other)
    got = [
        lax.ppermute(piece, "tensor", [(t, (t + 2 * step) % 8) for t in range(8)])
        for step, piece in zip(CHIP_STEPS, pieces)
    ]
    return finish(member[None].astype(jnp.int32), own, got, new_tokens)


def solution(mesh):
    placed = (
        P("section", None),
        P("section", None, None),
        P("section"),
        P(None, None, "section"),
        P(),
        P("section", "tensor"),
        P("section", "tensor"),
        P("tensor", "section"),
    )
    return jax.shard_map(
        on_device,
        mesh=mesh,
        in_specs=placed,
        out_specs=P(None, "tensor", "section"),
        check_vma=False,
    )
```

```python
import functools
import math

import jax
import jax.numpy as jnp
from jax import lax
from jax.experimental import pallas as pl
from jax.experimental.pallas import tpu as pltpu
from jax.sharding import PartitionSpec as P

D = 8192
HD = 128
GQ = 8
PAGE = 16
CAP = 8
SEQ_G = 8
SECTIONS = 16
GROUP_TOK = CAP * PAGE
ROWS = 2 * SEQ_G
DEPTH = D // SECTIONS
WQ = GQ * HD
WKV = 2 * HD
EXTRA = 128
ID_LANE = 8
POSITIONS = 136

EPS = 1e-05
ROPE_BASE = 500000.0
BF16 = jnp.bfloat16
F32 = jnp.float32


def params(mib=16):
    return pltpu.CompilerParams(vmem_limit_bytes=mib * 1024 * 1024)


def rotation_tables():
    half = HD // 2
    frequency = ROPE_BASE ** (-2.0 * jnp.arange(half, dtype=F32) / HD)
    angles = jnp.arange(POSITIONS, dtype=jnp.int32).astype(F32)[:, None] * frequency
    cosine, sine = jnp.cos(angles), jnp.sin(angles)
    return (
        jnp.concatenate([cosine, cosine], axis=-1),
        jnp.concatenate([-sine, sine], axis=-1),
    )


def turned(rows, cosine, sine):
    return rows * cosine + pltpu.roll(rows, HD // 2, 1) * sine


def shifted(array, axis, step):
    pairs = []
    for z in range(4):
        for x in range(4):
            for member in range(8):
                along_x = (axis + member) % 2 == 0
                to_z = z if along_x else (z + step) % 4
                to_x = (x + step) % 4 if along_x else x
                pairs.append(((z * 4 + x) * 8 + member, (to_z * 4 + to_x) * 8 + member))
    return lax.ppermute(array, ("section", "tensor"), pairs)


TILE = 256
PAGES = TILE // PAGE
EARLY_TILE = 128
EARLY_PAGES = EARLY_TILE // PAGE
BUFFERS = 6


def early_kernel(n_early, blocks_ref, order_ref, count_ref, x_ref, *refs):
    w_refs, refs = refs[: n_early // 2], refs[n_early // 2 :]
    acc_ref, middle_ref, late_ref, squares_ref, buf_ref, sems = refs
    count = count_ref[0]

    def copy(t, c):
        slot = t % BUFFERS
        row = pl.multiple_of(order_ref[t * EARLY_PAGES + c] * PAGE, PAGE)
        return pltpu.make_async_copy(
            x_ref.at[pl.ds(row, PAGE), :],
            buf_ref.at[slot, pl.ds(c * PAGE, PAGE), :],
            sems.at[slot, c],
        )

    def begin(t):
        for c in range(EARLY_PAGES):

            @pl.when(t * EARLY_PAGES + c < count)
            def _():
                copy(t, c).start()

    def end(t):
        for c in range(EARLY_PAGES):

            @pl.when(t * EARLY_PAGES + c < count)
            def _():
                copy(t, c).wait()

    for t in range(BUFFERS - 1):
        begin(t)

    def tile(t, _):
        begin(t + BUFFERS - 1)
        end(t)
        slot = t % BUFFERS
        rows = pl.ds(pl.multiple_of(t * EARLY_TILE, EARLY_TILE), EARLY_TILE)

        def depth(k):
            return pl.ds(pl.multiple_of(blocks_ref[k] * DEPTH, DEPTH), DEPTH)

        total = None
        for k in range(n_early):
            w = w_refs[k // 2][(k % 2) * DEPTH : (k % 2 + 1) * DEPTH, :]
            part = jnp.dot(buf_ref[slot, :, depth(k)], w, preferred_element_type=F32)
            total = part if total is None else total + part
        acc_ref[rows, :] = total
        for c in range(EARLY_PAGES):
            at = pl.ds(pl.multiple_of(t * EARLY_TILE + c * PAGE, PAGE), PAGE)
            sums = [None] * (DEPTH // 128)
            for k in range(SECTIONS):
                block = buf_ref[slot, c * PAGE : (c + 1) * PAGE, depth(k)]
                if k >= n_early:
                    rest_ref = middle_ref if k < n_early + 4 else late_ref
                    to = (k - n_early) % 4 * DEPTH
                    rest_ref[at, to : to + DEPTH] = block
                for j in range(len(sums)):
                    piece = block[:, j * 128 : (j + 1) * 128].astype(F32)
                    piece = piece * piece
                    sums[j] = piece if sums[j] is None else sums[j] + piece
            squares_ref[at, :] = (sums[0] + sums[1]) + (sums[2] + sums[3])
        return 0

    lax.fori_loop(0, pl.cdiv(count, EARLY_PAGES), tile, 0)


def kept(array):
    return pltpu.with_memory_space_constraint(array, pltpu.VMEM)


def in_hbm(array):
    return pltpu.with_memory_space_constraint(array, pltpu.HBM)


SMEM_SPEC = pl.BlockSpec(memory_space=pltpu.SMEM)
VMEM_SPEC = pl.BlockSpec(memory_space=pltpu.VMEM)


def prompt_early(blocks, order, count, x, weights):
    rows = x.shape[0]
    n_early = 2 * len(weights)
    return pl.pallas_call(
        functools.partial(early_kernel, n_early),
        in_specs=[SMEM_SPEC] * 3
        + [pl.BlockSpec(memory_space=pl.ANY)]
        + [VMEM_SPEC] * len(weights),
        out_specs=[VMEM_SPEC] * 4,
        out_shape=[
            pltpu.VMEM((rows, WKV), F32),
            pltpu.VMEM((rows, 4 * DEPTH), BF16),
            pltpu.VMEM((rows, 4 * DEPTH), BF16),
            pltpu.VMEM((rows, 128), F32),
        ],
        scratch_shapes=[
            pltpu.VMEM((BUFFERS, EARLY_TILE, D), BF16),
            pltpu.SemaphoreType.DMA((BUFFERS, EARLY_PAGES)),
        ],
        compiler_params=params(24),
        name="prompt_early",
    )(blocks, order, count, x, *weights)


def middle_kernel(count_ref, acc_ref, x_ref, *refs):
    w_refs, out_ref = refs[:-1], refs[-1]

    def tile(t, _):
        rows = pl.ds(pl.multiple_of(t * TILE, TILE), TILE)
        total = acc_ref[rows, :]
        for k, w_ref in enumerate(w_refs):
            x = x_ref[rows, k * 2 * DEPTH : (k + 1) * 2 * DEPTH]
            total = total + jnp.dot(x, w_ref[...], preferred_element_type=F32)
        out_ref[rows, :] = total
        return 0

    lax.fori_loop(0, pl.cdiv(count_ref[0], PAGES), tile, 0)


def prompt_middle(count, acc, x, weights):
    return pl.pallas_call(
        middle_kernel,
        in_specs=[SMEM_SPEC] + [VMEM_SPEC] * (2 + len(weights)),
        out_specs=VMEM_SPEC,
        out_shape=pltpu.VMEM(acc.shape, F32),
        compiler_params=params(8),
        name="prompt_middle",
    )(count, kept(acc), kept(x), *weights)


def late_kernel(
    order_ref, turn_ref, count_ref, cos_ref, sin_ref, acc_ref, rest_ref, squares_ref, *refs
):
    w_refs, pages_ref = refs[:-1], refs[-1]
    count = count_ref[0]
    pages_ref[...] = jnp.zeros_like(pages_ref)

    def tile(t, _):
        rows = pl.ds(pl.multiple_of(t * TILE, TILE), TILE)
        last = count - 1 - t * PAGES
        total = acc_ref[rows, :]
        for k, w_ref in enumerate(w_refs):
            x = rest_ref[rows, k * 2 * DEPTH : (k + 1) * 2 * DEPTH]
            total = total + jnp.dot(x, w_ref[...], preferred_element_type=F32)
        mean = jnp.sum(squares_ref[rows, :], axis=-1, keepdims=True) * (1.0 / D)
        total = total * lax.rsqrt(mean + EPS)
        for c in reversed(range(PAGES)):
            at = t * PAGES + jnp.minimum(c, last)
            turn = pl.ds(pl.multiple_of(turn_ref[at] * PAGE, PAGE), PAGE)
            slot = order_ref[at]
            to = pl.ds(pl.multiple_of((slot & (CAP - 1)) * PAGE, PAGE), PAGE)
            here = total[c * PAGE : (c + 1) * PAGE]
            key = turned(here[:, :HD], cos_ref[turn, :], sin_ref[turn, :])
            pages_ref[slot // CAP, to, :HD] = key.astype(BF16)
            pages_ref[slot // CAP, to, HD:] = here[:, HD:].astype(BF16)
        return 0

    lax.fori_loop(0, pl.cdiv(count, PAGES), tile, 0)


def prompt_late(order, turn, count, cosine, sine, early, weights):
    return pl.pallas_call(
        late_kernel,
        in_specs=[SMEM_SPEC] * 3 + [VMEM_SPEC] * (5 + len(weights)),
        out_specs=VMEM_SPEC,
        out_shape=jax.ShapeDtypeStruct((SECTIONS, GROUP_TOK, WKV), BF16),
        compiler_params=params(16),
        name="prompt_late",
    )(order, turn, count, cosine, sine, *[kept(array) for array in early], *weights)


def own_gain(gain_ref):
    section = lax.axis_index("section")
    return gain_ref[:, pl.ds(pl.multiple_of(section * DEPTH, DEPTH), DEPTH)]


def weight_kernel(gain_ref, kvw_ref, out_ref):
    column = jnp.broadcast_to(own_gain(gain_ref), (WKV, DEPTH)).T
    out_ref[...] = (kvw_ref[...].astype(F32) * column).astype(BF16)


def with_gain(gain, kv_weight):
    return pl.pallas_call(
        weight_kernel,
        out_shape=jax.ShapeDtypeStruct(kv_weight.shape, BF16),
        compiler_params=params(),
        name="with_gain",
    )(in_hbm(gain), in_hbm(kv_weight))


def project_kernel(
    slot_ref, tok_ref, gain_ref, qw_ref, kvw_ref, ids_ref, out_ref, order_ref, turn_ref, count_ref
):
    found = jnp.int32(0)
    for slot in range(SECTIONS * CAP):
        held = slot_ref[slot // CAP, slot % CAP]
        order_ref[found] = slot
        turn_ref[found] = jnp.maximum(held, 0) & (CAP - 1)
        found = found + jnp.where(held >= 0, 1, 0)
    count_ref[0] = found

    tok = tok_ref[...].astype(F32)
    scaled = (tok * own_gain(gain_ref)).astype(BF16)
    squares = jnp.sum(tok * tok, axis=-1, keepdims=True)
    high = squares.astype(BF16).astype(F32)
    low = squares - high
    q = jnp.dot(scaled, qw_ref[...], preferred_element_type=F32)
    kv = jnp.dot(scaled, kvw_ref[...], preferred_element_type=F32)
    lane = lax.broadcasted_iota(jnp.int32, (tok.shape[0], EXTRA), 1)
    extra = jnp.where(lane == 0, high, jnp.where(lane == 1, low, 0.0))
    half = tok.shape[0] // 2
    for g in range(SECTIONS):
        ids = ids_ref[g : g + 1, :]
        for array, at, width in ((q, 0, WQ), (kv, WQ, WKV), (extra, WQ + WKV, EXTRA)):
            rows = jnp.concatenate(
                [
                    array[g * SEQ_G : (g + 1) * SEQ_G],
                    array[half + g * SEQ_G : half + (g + 1) * SEQ_G],
                ],
                axis=0,
            )
            if width == EXTRA:
                rows = rows + ids
            out_ref[g, :, at : at + width] = rows.astype(BF16)


def project(own_ids, tokens, gain, q_weight, kv_weight, ids_wide):
    slots = jax.ShapeDtypeStruct((SECTIONS * CAP,), jnp.int32)
    return pl.pallas_call(
        project_kernel,
        in_specs=[SMEM_SPEC] + [VMEM_SPEC] * 5,
        out_specs=[VMEM_SPEC] + [SMEM_SPEC] * 3,
        out_shape=[
            jax.ShapeDtypeStruct((SECTIONS, ROWS, WQ + WKV + EXTRA), BF16),
            slots,
            slots,
            jax.ShapeDtypeStruct((1,), jnp.int32),
        ],
        compiler_params=params(),
        name="project",
    )(own_ids, in_hbm(tokens), gain, in_hbm(q_weight), kv_weight, ids_wide)


def ready_kernel(ctx_ref, got_ref, cos_ref, sin_ref, q_ref, key_ref, value_ref, seq_ref):
    got = got_ref[...].astype(F32)
    total = jnp.sum(got, axis=0)
    squares = (
        total[:, WQ + WKV : WQ + WKV + 1] + total[:, WQ + WKV + 1 : WQ + WKV + 2]
    )
    rscale = lax.rsqrt(squares * (1.0 / D) + EPS)
    total = total[:, : WQ + WKV] * rscale
    cosine = jnp.concatenate(
        [cos_ref[pl.ds(ctx_ref[r % SEQ_G] + r // SEQ_G, 1), :] for r in range(ROWS)], axis=0
    )
    sine = jnp.concatenate(
        [sin_ref[pl.ds(ctx_ref[r % SEQ_G] + r // SEQ_G, 1), :] for r in range(ROWS)], axis=0
    )
    for h in range(GQ):
        q_ref[h * ROWS : (h + 1) * ROWS, :] = turned(
            total[:, h * HD : (h + 1) * HD], cosine, sine
        ).astype(BF16)
    key_ref[...] = turned(total[:, WQ : WQ + HD], cosine, sine).astype(BF16)
    value_ref[...] = total[:, WQ + HD : WQ + WKV].astype(BF16)

    ids = jnp.max(got[:, :, WQ + WKV :], axis=1)
    lane_in = lax.broadcasted_iota(jnp.int32, (EXTRA, GROUP_TOK), 0)
    lane_out = lax.broadcasted_iota(jnp.int32, (EXTRA, GROUP_TOK), 1)
    spread = (lane_in == ID_LANE + lane_out // PAGE).astype(F32)
    ids = jnp.where(
        (lax.broadcasted_iota(jnp.int32, ids.shape, 1) >= ID_LANE), ids, 0.0
    )
    ids = jnp.dot(ids, spread, preferred_element_type=F32).astype(jnp.int32)
    position = (ids & (CAP - 1)) * PAGE + (
        lax.broadcasted_iota(jnp.int32, ids.shape, 1) & (PAGE - 1)
    )
    owner = jnp.full(ids.shape, -1, jnp.int32)
    for j in range(SEQ_G):
        held = (ids >= j * CAP) & (ids < (j + 1) * CAP) & (position < ctx_ref[j])
        owner = jnp.where(held, j, owner)
    seq_ref[...] = owner


def ready(context_len, got, cosine, sine):
    vmem = pl.BlockSpec(memory_space=pltpu.VMEM)
    return pl.pallas_call(
        ready_kernel,
        in_specs=[pl.BlockSpec(memory_space=pltpu.SMEM), vmem, vmem, vmem],
        out_shape=[
            jax.ShapeDtypeStruct((GQ * ROWS, HD), BF16),
            jax.ShapeDtypeStruct((ROWS, HD), BF16),
            jax.ShapeDtypeStruct((ROWS, HD), BF16),
            jax.ShapeDtypeStruct((SECTIONS, GROUP_TOK), jnp.int32),
        ],
        compiler_params=params(),
        name="ready",
    )(context_len, got, cosine, sine)


def attend_kernel(pages_ref, q_ref, key_ref, value_ref, seq_ref, ow_ref, out_ref, ow_out, sem):
    fetch = pltpu.make_async_copy(ow_ref, ow_out, sem)
    fetch.start()
    scale = 1.0 / math.sqrt(HD)
    q = q_ref[...]
    n = GQ * ROWS

    def against(keys):
        return (
            lax.dot_general(q, keys, (((1,), (1,)), ((), ())), preferred_element_type=F32) * scale
        )

    row = lax.broadcasted_iota(jnp.int32, (n, 1), 0)
    row_seq, row_step = row & (SEQ_G - 1), (row // SEQ_G) & 1
    col = lax.broadcasted_iota(jnp.int32, (n, ROWS), 1)
    fresh_ok = ((col & (SEQ_G - 1)) == row_seq) & (col // SEQ_G <= row_step)
    fresh = jnp.where(fresh_ok, against(key_ref[...]), -jnp.inf)
    cached = []
    peak = None
    for s in range(SECTIONS):
        ok = seq_ref[s : s + 1, :] == row_seq
        scores = jnp.where(ok, against(pages_ref[s, :, :HD]), -jnp.inf)
        cached.append(scores)
        peak = scores if peak is None else jnp.maximum(peak, scores)
    highest = jnp.maximum(
        jnp.max(peak, axis=-1, keepdims=True), jnp.max(fresh, axis=-1, keepdims=True)
    )
    fresh = jnp.exp(fresh - highest)
    cached = [jnp.exp(scores - highest) for scores in cached]
    denom = cached[0]
    for scores in cached[1:]:
        denom = denom + scores
    denom = jnp.sum(denom, axis=-1, keepdims=True) + jnp.sum(fresh, axis=-1, keepdims=True)
    inverse = 1.0 / denom
    mixed = jnp.dot(
        (fresh * inverse).astype(BF16), value_ref[...], preferred_element_type=F32
    )
    for s in range(SECTIONS):
        mixed = mixed + jnp.dot(
            (cached[s] * inverse).astype(BF16), pages_ref[s, :, HD:], preferred_element_type=F32
        )
    mixed = mixed.astype(BF16)
    for d in range(SECTIONS):
        for h in range(GQ):
            out_ref[d, :, h * HD : (h + 1) * HD] = mixed[h * ROWS : (h + 1) * ROWS]
    fetch.wait()


def attend(pages, q, key, value, seq, o_weight):
    return pl.pallas_call(
        attend_kernel,
        in_specs=[VMEM_SPEC] * 5 + [pl.BlockSpec(memory_space=pl.ANY)],
        out_specs=[VMEM_SPEC] * 2,
        out_shape=[
            jax.ShapeDtypeStruct((SECTIONS, ROWS, WQ), BF16),
            pltpu.VMEM(o_weight.shape, BF16),
        ],
        scratch_shapes=[pltpu.SemaphoreType.DMA(())],
        compiler_params=params(),
        name="attend",
    )(pages, q, key, value, seq, in_hbm(o_weight))


def output_kernel(attn_ref, ow_ref, mine_ref, other_ref, total_ref):
    core = lax.axis_index("tensor") % 2
    attn = attn_ref[...].reshape(SECTIONS * ROWS, WQ)
    part = jnp.dot(attn, ow_ref[...], preferred_element_type=F32)
    total_ref[...] = part.reshape(total_ref.shape)
    for chip in range(4):
        mine_ref[chip] = total_ref[2 * chip + core]
        other_ref[chip] = total_ref[2 * chip + 1 - core].astype(BF16)


def output_part(attn, o_weight):
    width = o_weight.shape[1]
    half = (4, 2 * ROWS, width)
    return pl.pallas_call(
        output_kernel,
        out_shape=[jax.ShapeDtypeStruct(half, F32), jax.ShapeDtypeStruct(half, BF16)],
        scratch_shapes=[pltpu.VMEM((8, 2 * ROWS, width), F32)],
        compiler_params=params(),
        name="output_part",
    )(attn, kept(o_weight))


CHIP_STEPS = (2, 1, 3)


def pair_kernel(mine_ref, got_ref, own_ref, *out_refs):
    chip = lax.axis_index("tensor") // 2

    def pair(at):
        return mine_ref[at] + got_ref[at].astype(F32)

    own_ref[...] = pair(chip)
    for step, out_ref in zip(CHIP_STEPS, out_refs):
        out_ref[...] = pair((chip + step) % 4).astype(BF16)


def pair_sums(mine, got):
    piece = mine.shape[1:]
    return pl.pallas_call(
        pair_kernel,
        out_shape=[jax.ShapeDtypeStruct(piece, F32)] + [jax.ShapeDtypeStruct(piece, BF16)] * 3,
        compiler_params=params(),
        name="pair_sums",
    )(mine, got)


def finish_kernel(_, own_ref, a_ref, b_ref, c_ref, tok_ref, out_ref):
    total = own_ref[...]
    for got_ref in (a_ref, b_ref, c_ref):
        total = total + got_ref[...].astype(F32)
    tok = tok_ref[...].astype(F32)
    for i in range(2):
        rows = jnp.concatenate(
            [total[g * ROWS + i * SEQ_G : g * ROWS + (i + 1) * SEQ_G] for g in range(2)], axis=0
        )
        out_ref[i] = (tok[i] + rows).astype(BF16)


def finish(member, own, got, tokens):
    rows, width = own.shape
    block = pl.BlockSpec((2, rows // 2, width), lambda r, member: (0, member[0], 0))
    whole = pl.BlockSpec((rows, width), lambda r, member: (0, 0))
    return pl.pallas_call(
        finish_kernel,
        grid_spec=pltpu.PrefetchScalarGridSpec(
            num_scalar_prefetch=1,
            grid=(1,),
            in_specs=[whole] * 4 + [block],
            out_specs=pl.BlockSpec((2, rows // 2, width), lambda r, member: (0, 0, 0)),
        ),
        out_shape=jax.ShapeDtypeStruct((2, rows // 2, width), BF16),
        compiler_params=params(),
        name="finish",
    )(member, own, *got, tokens)


def on_device(
    prompt_rows, page_slot, context_len, new_tokens, norm_gain, q_weight, kv_weight, o_weight
):
    section = lax.axis_index("section")
    member = lax.axis_index("tensor")
    core = member % 2
    own_ids = page_slot[0]
    cosine, sine = rotation_tables()

    ids_wide = jnp.pad(own_ids.astype(F32), ((0, 0), (ID_LANE, EXTRA - ID_LANE - CAP)))
    payload, order, turn, count = project(
        own_ids, new_tokens.reshape(-1, DEPTH), norm_gain[None, :], q_weight, kv_weight, ids_wide
    )

    weight = with_gain(norm_gain[None, :], kv_weight)
    from_1 = shifted(weight, 0, 1)
    from_3 = shifted(weight, 0, -1)
    from_2 = shifted(weight, 0, 2)
    near = jnp.concatenate([weight, from_1], axis=0)
    far = jnp.concatenate([from_3, from_2], axis=0)
    near, far, payload = lax.optimization_barrier((near, far, payload))
    got = lax.all_to_all(payload, "section", split_axis=0, concat_axis=0, tiled=True)
    near_p = shifted(near, 1, 1)
    far_m = shifted(far, 1, -1)
    far_p = shifted(far, 1, 1)
    near_m = shifted(near, 1, -1)
    near_o = shifted(near_p, 1, 1)
    far_o = shifted(far_m, 1, -1)

    def blocks(*steps):
        z, x = section // 4, section % 4
        ids = []
        for a, b in steps:
            at_0 = ((z + b) % 4) * 4 + (x + a) % 4
            at_1 = ((z + a) % 4) * 4 + (x + b) % 4
            ids.append(jnp.where(core == 0, at_0, at_1))
        return jnp.stack(ids).astype(jnp.int32)

    where = blocks(
        (0, 0), (3, 0), (1, 0), (2, 0),
        (0, 3), (3, 3), (1, 1), (2, 1),
        (0, 1), (3, 1), (1, 3), (2, 3),
        (0, 2), (3, 2), (1, 2), (2, 2),
    )
    acc, x_middle, x_late, squares = prompt_early(
        where, order, count, prompt_rows, (near, far, near_p, far_m)
    )
    acc = prompt_middle(count, acc, x_middle, (near_m, far_p))
    pages = prompt_late(
        order, turn, count, cosine, sine, (acc, x_late, squares), (near_o, far_o)
    )
    queries, new_keys, new_values, owners = ready(context_len, got, cosine, sine)
    received = lax.all_to_all(pages, "section", split_axis=0, concat_axis=0, tiled=True)
    attn, o_weight = attend(received, queries, new_keys, new_values, owners, o_weight)
    attn = lax.all_to_all(attn, "section", split_axis=0, concat_axis=0, tiled=True)
    mine, other = output_part(attn, o_weight)
    other = lax.ppermute(other, "tensor", [(t, t ^ 1) for t in range(8)])
    own, *pieces = pair_sums(mine, other)
    got = [
        lax.ppermute(piece, "tensor", [(t, (t + 2 * step) % 8) for t in range(8)])
        for step, piece in zip(CHIP_STEPS, pieces)
    ]
    return finish(member[None].astype(jnp.int32), own, got, new_tokens)


def solution(mesh):
    placed = (
        P("section", None),
        P("section", None, None),
        P("section"),
        P(None, None, "section"),
        P(),
        P("section", "tensor"),
        P("section", "tensor"),
        P("tensor", "section"),
    )
    return jax.shard_map(
        on_device,
        mesh=mesh,
        in_specs=placed,
        out_specs=P(None, "tensor", "section"),
        check_vma=False,
    )
```
